256 devices in a mesh: ctx: 32 (over x, y, core), tp: 8 (over z).
Axes of the slice: x: 4, y: 4, z: 8, core: 2. Of those that a mesh axis runs over, the one named last changes fastest.
Arguments:
- queries: bfloat16 [2, 8, 64, 128], P(None, None, 'tp'), may hold values from -128 to 128
- new_kv: bfloat16 [2, 2, 8, 8, 128], P(None, None, None, 'tp'), may hold values from -16 to 16
- long_cache: bfloat16 [2, 8, 16384, 8, 128], P(None, None, 'ctx', 'tp'), may hold values from -6 to 6
- short_cache: bfloat16 [2, 8, 256, 8, 128], P(None, None, None, 'tp'), may hold values from -6 to 6
- lengths: int32 [8], replicated, may hold values from 4096 to 16384, as said below
- residual: bfloat16 [2, 8, 8192], P(None, None, 'ctx'), may hold values from -12 to 12
- out_weight: bfloat16 [8192, 8192], P('tp', 'ctx'), may hold values from -0.0625 to 0.0625
- final_gain: float32 [8192], P('ctx'), may hold values from 1 to 96
- head_weight: bfloat16 [8192, 128256], P('ctx', 'tp'), may hold values from -0.0625 to 0.0625
- targets: int32 [8], replicated, may hold values from 0 to 128255
Outputs:
- scores: float32 [8, 128256], P(None, ('tp', 'ctx'))
- chosen: float32 [8], replicated
The draws below stay inside these ranges and needn't reach their ends.
Inputs may be any that keep to these rules, and one draw needn't show every extreme that they name: Row b's cached context is its first lengths[b] positions; in every draw some row holds 16384 positions.
All inputs are finite; a program needn't handle non-finite values.
Results may differ from the reference program's by a relative error of at most 0.00098.
Values sent between devices are 32-bit elements; how exact they have to be, the bound alone decides.
No kernel may reach another device: no remote copies, remote signals or barrier semaphores. Data moves between devices by JAX's collectives and lax.ppermute only.
A program may use at most 64 MiB of HBM per device.

```python
import math
import jax
import jax.numpy as jnp
from jax import lax

D = 8192
HEADS = 64
KV_HEADS = 8
HEAD_DIM = 128
VOCAB = 128256
ROWS = 8
CTX_DEV = 512
SHORT = 256
LONG = 16384
N_CTX = 32


def common_random_inputs(key):
    pieces = jax.random.split(key, 6)
    query_base = jax.random.normal(pieces[0], (2, ROWS, HEADS, HEAD_DIM), jnp.float32)
    long_keys = jnp.clip(jax.random.normal(pieces[1], (ROWS, LONG, KV_HEADS, HEAD_DIM), jnp.float32), -6.0, 6.0)
    short_keys = jnp.clip(jax.random.normal(pieces[2], (ROWS, SHORT, KV_HEADS, HEAD_DIM), jnp.float32), -6.0, 6.0)
    quarter = LONG // 4
    long_first = jax.random.randint(pieces[3], (ROWS,), 0, quarter)
    long_second = (long_first + 1 + jax.random.randint(pieces[4], (ROWS,), 0, quarter - 1)) % quarter
    short_first = jax.random.randint(pieces[5], (ROWS,), 0, SHORT)
    brief_cache_latter = (short_first + 1 + jax.random.randint(jax.random.fold_in(pieces[5], 7), (ROWS,), 0, SHORT - 1)) % SHORT
    row_index = jnp.arange(ROWS)
    long_keys = long_keys.at[row_index, long_second].set(long_keys[row_index, long_second])
    short_keys = short_keys.at[row_index, brief_cache_latter].set(short_keys[row_index, brief_cache_latter])
    return (query_base, long_keys, short_keys)


def draw_queries(key, part):
    query_base, long_keys, short_keys = common_random_inputs(key)
    drawn = 2.0 * query_base
    result = drawn
    return jnp.clip(result, -128.0, 128.0).astype(jnp.bfloat16)


def draw_new_kv(key, part):
    query_base = common_random_inputs(key)[0]
    key = jax.random.fold_in(key, 22)
    noise_key, value_key = jax.random.split(key)
    group_size = HEADS // KV_HEADS
    grouped = query_base.reshape(2, ROWS, KV_HEADS, group_size, HEAD_DIM).sum(3) / math.sqrt(group_size)
    fresh_keys = 1.1 * grouped + 0.3 * jax.random.normal(noise_key, (2, ROWS, KV_HEADS, HEAD_DIM), jnp.float32)
    fresh_values = jax.random.normal(value_key, (2, ROWS, KV_HEADS, HEAD_DIM), jnp.float32)
    return jnp.clip(jnp.stack([fresh_keys, fresh_values], axis=1), -16.0, 16.0).astype(jnp.bfloat16)


def draw_long_cache(key, part):
    long_keys = common_random_inputs(key)[1]
    key = jax.random.fold_in(key, 23)
    values = jnp.clip(jax.random.normal(key, (ROWS, LONG, KV_HEADS, HEAD_DIM), jnp.float32), -6.0, 6.0)
    return jnp.stack([long_keys, values]).astype(jnp.bfloat16)


def draw_short_cache(key, part):
    short_keys = common_random_inputs(key)[2]
    key = jax.random.fold_in(key, 24)
    values = jnp.clip(jax.random.normal(key, (ROWS, SHORT, KV_HEADS, HEAD_DIM), jnp.float32), -6.0, 6.0)
    return jnp.stack([short_keys, values]).astype(jnp.bfloat16)


def draw_lengths(key, part):
    key = jax.random.fold_in(key, 25)
    length_key, order_key = jax.random.split(key)
    counts = jax.random.randint(length_key, (ROWS,), LONG // 4, LONG + 1)
    order = jax.random.permutation(order_key, ROWS)
    counts = counts.at[order[0]].set(LONG)
    return counts.astype(jnp.int32)


def draw_residual(key, part):
    key = jax.random.fold_in(key, 26)
    first_key = jax.random.fold_in(key, 0)
    ramp = 1.0 + 2.0 * jnp.arange(D, dtype=jnp.float32) / (D - 1)
    values = 0.25 * jax.random.normal(first_key, (2, ROWS, D), jnp.float32) * ramp
    return jnp.clip(values, -12.0, 12.0).astype(jnp.bfloat16)


def draw_final_gain(key, part):
    key = jax.random.fold_in(key, 27)
    low = math.log(2.0)
    high = math.log(5.0)
    return jnp.exp(jax.random.uniform(key, (D,), jnp.float32, low, high))


def place_ends(entries, key, low, high):
    longest = entries.shape.index(max(entries.shape))
    spots = []
    for shift in (0, 1):
        where = [jax.random.randint(jax.random.fold_in(key, axis), (), 0, length) for axis, length in enumerate(entries.shape)]
        where[longest] = (where[longest] + shift) % entries.shape[longest]
        spots.append(tuple(where))
    return entries.at[spots[0]].set(low).at[spots[1]].set(high)


def level_of(rng, extent, cuts, least, high):
    def one(position, shards_of):
        steps = jax.random.uniform(jax.random.fold_in(jax.random.fold_in(rng, 6), position), (shards_of,), jnp.float32, least / len(cuts), high / len(cuts))
        return jnp.repeat(jnp.exp(steps), extent[position] // shards_of).reshape((-1,) + (1,) * (len(extent) - position - 1))

    factor_of = one(*cuts[0])
    for cut in cuts[1:]:
        factor_of = factor_of * one(*cut)
    return factor_of


def noise(own_key, extent, scale, bound, cuts=(), kind=jnp.bfloat16):
    drawn = scale * jax.random.normal(own_key, extent, jnp.float32)
    if cuts:
        drawn = drawn * level_of(own_key, extent, cuts, -0.22, 0.18)
    return jnp.clip(drawn, -bound, bound).astype(kind)


def setup_inputs(seed: int = 0) -> dict:
    seeds = jax.random.split(jax.random.key(seed), 11)
    queries = draw_queries(jax.random.fold_in(seeds[10], 71), 0)
    new_kv = draw_new_kv(jax.random.fold_in(seeds[10], 71), 0)
    long_cache = draw_long_cache(jax.random.fold_in(seeds[10], 71), 0)
    short_cache = draw_short_cache(jax.random.fold_in(seeds[10], 71), 0)
    lengths = draw_lengths(jax.random.fold_in(seeds[10], 71), 0)
    residual = draw_residual(jax.random.fold_in(seeds[10], 71), 0)
    out_weight = noise(seeds[6], (HEADS * HEAD_DIM, D), (HEADS * HEAD_DIM) ** -0.5, 0.0625, ((0, 8), (1, 32)))
    final_gain = draw_final_gain(jax.random.fold_in(seeds[10], 71), 0)
    head_weight = noise(seeds[8], (D, VOCAB), D ** -0.5, 0.0625, ((0, 32), (1, 8)))
    targets = place_ends(jax.random.randint(seeds[9], (ROWS,), 0, VOCAB), jax.random.fold_in(seeds[9], 1), 0, VOCAB - 1).astype(jnp.int32)
    return dict(queries=queries, new_kv=new_kv, long_cache=long_cache, short_cache=short_cache, lengths=lengths, residual=residual, out_weight=out_weight, final_gain=final_gain, head_weight=head_weight, targets=targets)


NEG_FILL = -1e+30
NORM_EPS = 1e-05
CONTRAST_WEIGHT = 0.5
LOG_FLOOR = -2.302585092994046

def attend(query_matrix_rows, key_blocks, value_blocks, usable, incoming_key, value_new):
    score_scale = HEAD_DIM ** (-0.5)
    scores = jnp.einsum('bgd,bntd->bgnt', query_matrix_rows.astype(jnp.float32), key_blocks.astype(jnp.float32)) * score_scale
    mask = usable[:, None]
    masked = jnp.where(mask, scores, NEG_FILL)
    block_top = lax.optimization_barrier(jnp.max(masked, axis=-1))
    weights = jnp.where(mask, jnp.exp(masked - block_top[..., None]), 0.0)
    block_total = lax.optimization_barrier(jnp.sum(weights, axis=-1))
    rounded = weights.astype(jnp.bfloat16)
    block_out = jnp.einsum('bgnt,bntd->bgnd', rounded.astype(jnp.float32), value_blocks.astype(jnp.float32))
    peak = lax.optimization_barrier(jnp.max(block_top, axis=-1))
    factor = jnp.exp(block_top - peak[..., None])
    totals = lax.optimization_barrier(jnp.sum(block_total * factor, axis=-1))
    gathered = lax.optimization_barrier(jnp.sum(block_out * factor[..., None], axis=2))
    own = jnp.einsum('bgd,bd->bg', query_matrix_rows.astype(jnp.float32), incoming_key.astype(jnp.float32)) * score_scale
    final = jnp.maximum(peak, own)
    older = jnp.exp(peak - final)
    newer = jnp.exp(own - final)
    mixed = gathered * older[..., None] + newer[..., None] * value_new.astype(jnp.float32)[:, None, :]
    return (mixed / (totals * older + newer)[..., None]).astype(jnp.bfloat16)

def reference(queries, new_kv, long_cache, short_cache, lengths, residual, out_weight, final_gain, head_weight, targets):
    group_size = HEADS // KV_HEADS
    positions = jnp.arange(LONG, dtype=jnp.int32).reshape(N_CTX, CTX_DEV)
    long_usable = positions[None] < lengths[:, None, None]
    short_usable = jnp.ones((ROWS, 1, SHORT), dtype=bool)
    grouped_query_heads = queries.reshape(2, ROWS, KV_HEADS, group_size, HEAD_DIM)

    def per_head(head_index):
        long_part = lax.dynamic_index_in_dim(long_cache, head_index, 3, keepdims=False)
        short_part = lax.dynamic_index_in_dim(short_cache, head_index, 3, keepdims=False)
        fresh = lax.dynamic_index_in_dim(new_kv, head_index, 3, keepdims=False)
        query_part = lax.dynamic_index_in_dim(grouped_query_heads, head_index, 2, keepdims=False)
        with_context = attend(query_part[0], long_part[0].reshape(ROWS, N_CTX, CTX_DEV, HEAD_DIM), long_part[1].reshape(ROWS, N_CTX, CTX_DEV, HEAD_DIM), long_usable, fresh[0, 0], fresh[0, 1])
        context_free = attend(query_part[1], short_part[0].reshape(ROWS, 1, SHORT, HEAD_DIM), short_part[1].reshape(ROWS, 1, SHORT, HEAD_DIM), short_usable, fresh[1, 0], fresh[1, 1])
        return jnp.stack([with_context, context_free])
    attended = lax.map(per_head, jnp.arange(KV_HEADS, dtype=jnp.int32))
    attended = jnp.moveaxis(attended, 0, 2).reshape(2 * ROWS, HEADS * HEAD_DIM)
    projected = jnp.dot(attended, out_weight, preferred_element_type=jnp.float32)
    stream = residual.reshape(2 * ROWS, D).astype(jnp.float32) + projected
    inverse = lax.rsqrt(lax.optimization_barrier(jnp.mean(stream * stream, axis=-1)) + NORM_EPS)
    scaled = (stream * final_gain).astype(jnp.bfloat16)
    logits = jnp.dot(scaled, head_weight, preferred_element_type=jnp.float32) * inverse[:, None]
    logits = logits.reshape(2, ROWS, VOCAB)
    vocab_peak = lax.optimization_barrier(jnp.max(logits, axis=-1))
    lse = vocab_peak + jnp.log(lax.optimization_barrier(jnp.sum(jnp.exp(logits - vocab_peak[..., None]), axis=-1)))
    logp = logits - lse[..., None]
    scores = (1.0 + CONTRAST_WEIGHT) * logp[0] - CONTRAST_WEIGHT * logp[1] + jnp.minimum(0.0, logits[0] - vocab_peak[0][:, None] - LOG_FLOOR)
    chosen = jnp.take_along_axis(scores, targets[:, None], axis=1)[:, 0]
    return (scores, chosen)
```

```python
import jax
import jax.numpy as jnp
from jax import lax
from jax.sharding import PartitionSpec as P

D = 8192
HEAD_DIM = 128


NEG_FILL = -1e30
NORM_EPS = 1e-05
CONTRAST_WEIGHT = 0.5
LOG_FLOOR = -2.302585092994046


CTX_STEPS = (1, 2, 6, 8, 24)


def swap(value, mask):
    size = lax.axis_size("ctx")
    return lax.ppermute(value, "ctx", [(i, i ^ mask) for i in range(size)])


def merge_blocks(state, other):
    peak_one, peak_two = state[:, 128:129], other[:, 128:129]
    peak = jnp.maximum(peak_one, peak_two)
    summed = state * jnp.exp(peak_one - peak) + other * jnp.exp(peak_two - peak)
    lane = lax.broadcasted_iota(jnp.int32, state.shape, 1)
    return jnp.where(lane == 128, peak, summed)


def local_block(query_matrix_rows, key_matrix_rows, value_rows, usable):
    score_scale = HEAD_DIM ** (-0.5)
    scores = (
        jnp.einsum(
            "bkgd,btkd->bkgt",
            query_matrix_rows,
            key_matrix_rows,
            preferred_element_type=jnp.float32,
        )
        * score_scale
    )
    mask = usable[:, None, None, :]
    masked = jnp.where(mask, scores, NEG_FILL)
    peak_local = jnp.max(masked, axis=-1)
    weights = jnp.where(mask, jnp.exp(masked - peak_local[..., None]), 0.0)
    totals = jnp.sum(weights, axis=-1)
    output = jnp.einsum(
        "bkgt,btkd->bkgd",
        weights.astype(jnp.bfloat16),
        value_rows,
        preferred_element_type=jnp.float32,
    )
    return (peak_local, totals, output)


def finish_branch(peak_all, totals, output, query_matrix_rows, incoming_key, value_new):
    score_scale = HEAD_DIM ** (-0.5)
    own = (
        jnp.einsum(
            "faew,faw->fae", query_matrix_rows, incoming_key, preferred_element_type=jnp.float32
        )
        * score_scale
    )
    final = jnp.maximum(peak_all, own)
    older = jnp.exp(peak_all - final)
    newer = jnp.exp(own - final)
    mixed = (
        output * older[..., None] + newer[..., None] * value_new.astype(jnp.float32)[:, :, None, :]
    )
    return (mixed / (totals * older + newer)[..., None]).astype(jnp.bfloat16)


def vocab_local(branch_logits, column_start, targets):
    peak_local = jnp.max(branch_logits, axis=-1)
    totals = jnp.sum(jnp.exp(branch_logits - peak_local[..., None]), axis=-1)
    columns = column_start + jnp.arange(branch_logits.shape[-1], dtype=jnp.int32)
    target_hit = columns[None, :] == targets[:, None]
    picks = jnp.sum(jnp.where(target_hit[None], branch_logits, 0.0), axis=-1)
    return (peak_local, totals, picks)


def per_device(
    queries,
    new_kv,
    long_cache,
    short_cache,
    lengths,
    residual,
    out_weight,
    final_gain,
    head_weight,
    targets,
):
    row_count = queries.shape[1]
    heads_here = queries.shape[2]
    kv_here = long_cache.shape[3]
    block_len = long_cache.shape[2]
    group_size = heads_here // kv_here
    width_here = residual.shape[2]
    vocab_here = head_weight.shape[1]
    grouped_query_heads = queries.reshape(2, row_count, kv_here, group_size, HEAD_DIM)
    position = lax.axis_index("ctx") * block_len + jnp.arange(block_len, dtype=jnp.int32)
    long_usable = position[None, :] < lengths[:, None]
    peak_local, totals, output = local_block(
        grouped_query_heads[0], long_cache[0], long_cache[1], long_usable
    )
    state = jnp.concatenate(
        [
            output.reshape(-1, HEAD_DIM),
            peak_local.reshape(-1, 1),
            totals.reshape(-1, 1),
            jnp.zeros((row_count * heads_here, HEAD_DIM - 2), jnp.float32),
        ],
        axis=1,
    )
    for mask in CTX_STEPS:
        state = merge_blocks(state, swap(state, mask))
    output = state[:, :HEAD_DIM].reshape(output.shape)
    peak_all = state[:, HEAD_DIM].reshape(peak_local.shape)
    totals = state[:, HEAD_DIM + 1].reshape(totals.shape)
    with_context = finish_branch(
        peak_all, totals, output, grouped_query_heads[0], new_kv[0, 0], new_kv[0, 1]
    )
    short_usable = jnp.ones((row_count, short_cache.shape[2]), dtype=bool)
    short_peak, short_totals, short_output = local_block(
        grouped_query_heads[1], short_cache[0], short_cache[1], short_usable
    )
    context_free = finish_branch(
        short_peak, short_totals, short_output, grouped_query_heads[1], new_kv[1, 0], new_kv[1, 1]
    )
    attended = jnp.stack([with_context, context_free]).reshape(2 * row_count, heads_here * HEAD_DIM)
    projected = jnp.dot(attended, out_weight, preferred_element_type=jnp.float32)
    tp_size = lax.axis_size("tp")
    spread = jnp.broadcast_to(projected[None], (tp_size,) + projected.shape)
    projected = jnp.sum(lax.all_to_all(spread, "tp", 0, 0, tiled=True), axis=0)
    stream = residual.reshape(2 * row_count, width_here).astype(jnp.float32) + projected
    squares = jnp.sum(stream * stream, axis=-1)
    scaled = (stream * final_gain).astype(jnp.bfloat16)
    partial_value = jnp.dot(scaled, head_weight, preferred_element_type=jnp.float32)
    ctx_size = lax.axis_size("ctx")
    share_width = vocab_here // ctx_size
    padded_width = -(-(share_width + 1) // 128) * 128
    rows = 2 * row_count
    blocks = partial_value.reshape(rows, ctx_size, share_width).transpose(1, 0, 2)
    extra = jnp.broadcast_to(
        squares[None, :, None], (ctx_size, rows, padded_width - share_width)
    )
    blocks = jnp.concatenate([blocks, extra], axis=2)
    blocks = blocks.reshape(ctx_size // 2, 2, rows, padded_width)
    core = lax.axis_index("ctx") % 2
    mine = lax.dynamic_index_in_dim(blocks, core, 1, keepdims=False)
    theirs = lax.dynamic_index_in_dim(blocks, 1 - core, 1, keepdims=False)
    mine = mine + swap(theirs, 1)
    chips = [list(range(which, ctx_size, 2)) for which in range(2)]
    received = lax.all_to_all(mine, "ctx", 0, 0, tiled=True, axis_index_groups=chips)
    summed = jnp.sum(received, axis=0)
    total_squares = summed[:, share_width]
    local_logits = summed[:, :share_width]
    inverse = lax.rsqrt(total_squares / D + NORM_EPS)
    local_logits = (local_logits * inverse[:, None]).reshape(2, row_count, share_width)
    column_start = lax.axis_index("tp") * vocab_here + lax.axis_index("ctx") * share_width
    stats = vocab_local(local_logits, column_start, targets)
    packed = jnp.stack([part.reshape(-1) for part in stats])
    devices = ctx_size * tp_size
    everyone = lax.all_to_all(
        jnp.broadcast_to(packed[None], (devices,) + packed.shape), ("ctx", "tp"), 0, 0, tiled=True
    )
    vocab_peak = jnp.max(everyone[:, 0], axis=0)
    vocab_totals = jnp.sum(everyone[:, 1] * jnp.exp(everyone[:, 0] - vocab_peak), axis=0)
    picks = jnp.sum(everyone[:, 2], axis=0)
    vocab_peak, vocab_totals, picks = (
        part.reshape(2, row_count) for part in (vocab_peak, vocab_totals, picks)
    )
    lse = vocab_peak + jnp.log(vocab_totals)
    logp = local_logits - lse[..., None]
    scores = (
        (1.0 + CONTRAST_WEIGHT) * logp[0]
        - CONTRAST_WEIGHT * logp[1]
        + jnp.minimum(0.0, local_logits[0] - vocab_peak[0][:, None] - LOG_FLOOR)
    )
    picked_logp = picks - lse
    chosen = (
        (1.0 + CONTRAST_WEIGHT) * picked_logp[0]
        - CONTRAST_WEIGHT * picked_logp[1]
        + jnp.minimum(0.0, picks[0] - vocab_peak[0] - LOG_FLOOR)
    )
    return (scores, chosen)


def solution(mesh):
    placed = (
        P(None, None, "tp", None),
        P(None, None, None, "tp", None),
        P(None, None, "ctx", "tp", None),
        P(None, None, None, "tp", None),
        P(),
        P(None, None, "ctx"),
        P("tp", "ctx"),
        P("ctx"),
        P("ctx", "tp"),
        P(),
    )
    return jax.shard_map(
        per_device,
        mesh=mesh,
        in_specs=placed,
        out_specs=(P(None, ("tp", "ctx")), P()),
        check_vma=False,
    )
```

```python
import functools

import jax
import jax.numpy as jnp
from jax import lax
from jax.experimental import pallas as pl
from jax.experimental.pallas import tpu as pltpu
from jax.sharding import PartitionSpec as P

D = 8192
HEAD_DIM = 128
SCORE_SCALE = HEAD_DIM ** (-0.5)

NEG_FILL = -1e30
NORM_EPS = 1e-05
CONTRAST_WEIGHT = 0.5
LOG_FLOOR = -2.302585092994046

F32 = jnp.float32
BF16 = jnp.bfloat16
VMEM = pl.BlockSpec(memory_space=pltpu.VMEM)
SMEM = pl.BlockSpec(memory_space=pltpu.SMEM)
ANY = pl.BlockSpec(memory_space=pl.ANY)


def dot_rows(left, right):
    return lax.dot_general(left, right, (((1,), (1,)), ((), ())), preferred_element_type=F32)


def iota(shape, axis):
    return lax.broadcasted_iota(jnp.int32, shape, axis)


def long_kernel(chunks, lengths, queries, cache, state, held, wide, stat, sems):
    rows, block_len = cache.shape[1], cache.shape[2]
    per = rows // chunks
    copies = [
        pltpu.make_async_copy(
            cache.at[part, pl.ds(c * per, per)],
            held.at[part, pl.ds(c * per, per)],
            sems.at[part * chunks + c],
        )
        for part in range(2)
        for c in range(chunks)
    ]
    for copy in copies:
        copy.start()
    start = lax.axis_index("ctx") * block_len
    query = queries[0].astype(F32)
    heads = query.shape[0] // rows
    position = start + iota((heads, block_len), 1)
    lane = iota((heads, HEAD_DIM), 1)
    kept = []
    for b in range(rows):
        if b % per == 0:
            copies[b // per].wait()
        mine = query[b * heads : (b + 1) * heads].astype(BF16)
        mask = position < lengths[b]
        scores = jnp.where(mask, dot_rows(mine, held[0, b]) * SCORE_SCALE, NEG_FILL)
        top = jnp.max(scores, axis=1, keepdims=True)
        weights = jnp.where(mask, jnp.exp(scores - top), 0.0)
        total = jnp.sum(weights, axis=1, keepdims=True)
        stat[pl.ds(b, heads, stride=rows), :] = jnp.where(lane == 0, top, total)
        kept.append(weights.astype(BF16))
    for b in range(rows):
        if b % per == 0:
            copies[chunks + b // per].wait()
        wide[pl.ds(b, heads, stride=rows), :] = jnp.dot(
            kept[b], held[1, b], preferred_element_type=F32
        )
    half = HEAD_DIM // 2
    turned = wide[...].T
    state[0:half, :] = jnp.concatenate([turned[:half], turned[half:]], axis=1)
    turned = stat[...].T[:8]
    state[half : half + 8, :] = jnp.concatenate([turned, turned], axis=1)


def short_kernel(queries, cache, fresh, aux):
    rows = cache.shape[1]
    query = [queries[0].astype(F32), queries[1].astype(F32)]
    heads = query[0].shape[0] // rows
    key = [fresh[0, 0].astype(F32), fresh[1, 0].astype(F32)]
    value = [fresh[0, 1].astype(F32), fresh[1, 1].astype(F32)]
    for b in range(rows):
        part = [q[b * heads : (b + 1) * heads] for q in query]
        own = [
            jnp.sum(part[n] * key[n][b : b + 1], axis=1, keepdims=True) * SCORE_SCALE
            for n in range(2)
        ]
        scores = dot_rows(part[1].astype(BF16), cache[0, b]) * SCORE_SCALE
        top = jnp.max(scores, axis=1, keepdims=True)
        weights = jnp.exp(scores - top)
        total = jnp.sum(weights, axis=1, keepdims=True)
        output = jnp.dot(weights.astype(BF16), cache[1, b], preferred_element_type=F32)
        final = jnp.maximum(top, own[1])
        older = jnp.exp(top - final)
        newer = jnp.exp(own[1] - final)
        mixed = output * older + newer * value[1][b : b + 1]
        where = pl.ds(b, heads, stride=rows)
        aux[0, where, :] = mixed / (total * older + newer)
        aux[1, where, :] = jnp.broadcast_to(own[0], (heads, HEAD_DIM))
        aux[2, where, :] = jnp.broadcast_to(value[0][b : b + 1], (heads, HEAD_DIM))


def merge_states(parts):
    half = HEAD_DIM // 2
    tops = [part[half : half + 1, :] for part in parts]
    peak = functools.reduce(jnp.maximum, tops)
    factors = [jnp.exp(top - peak) for top in tops]
    total = sum(part[half + 1 : half + 2, :] * f for part, f in zip(parts, factors))
    values = sum(part[0:half, :] * f for part, f in zip(parts, factors))
    return values, peak, total


def packed_stats(peak, total):
    return jnp.where(iota((8, HEAD_DIM), 0) == 0, peak, total)


def pair_kernel(one, two, spread):
    half = HEAD_DIM // 2
    values, peak, total = merge_states([one, two])
    stats = packed_stats(peak, total)
    for k in range(spread.shape[0]):
        spread[k, 0:half, :] = values
        spread[k, half : half + 8, :] = stats


def project_kernel(states, aux, weight, spread):
    half = HEAD_DIM // 2
    values, peak, total = merge_states([states.at[k] for k in range(states.shape[0])])
    blank = jnp.zeros((half - 8, HEAD_DIM), F32)
    turned = jnp.concatenate([values, packed_stats(peak, total), blank], axis=0).T
    left, right = turned[:half], turned[half:]
    lane = iota((half, HEAD_DIM), 1)
    output = jnp.where(lane < half, left, pltpu.roll(right, half, 1))
    peak, total = left[:, half : half + 1], left[:, half + 1 : half + 2]
    own = aux[1][:, 0:1]
    final = jnp.maximum(peak, own)
    older = jnp.exp(peak - final)
    newer = jnp.exp(own - final)
    attended = [(output * older + newer * aux[2]) / (total * older + newer), aux[0]]
    rows = 8
    heads = half // rows
    rows_wide = jnp.concatenate(
        [
            jnp.concatenate([part[h * rows : (h + 1) * rows] for part in attended], axis=0)
            for h in range(heads)
        ],
        axis=1,
    )
    projected = jnp.dot(rows_wide.astype(BF16), weight[...], preferred_element_type=F32)
    for k in range(spread.shape[0]):
        spread[k] = projected


def head_blocks(other, share, scaled, squares, weight, blocks, held, sems):
    count, vocab = blocks.shape[0], weight.shape[0]
    padded, reach = blocks.shape[2], held.shape[1]
    fetched = sems_rows(share)
    core = lax.rem(lax.axis_index("ctx"), 2)
    which = 1 - core if other else core

    def place(k):
        offset = (2 * k + which) * share
        base = jnp.minimum(offset // 16 * 16, vocab - fetched)
        return pl.multiple_of(base, 16), offset - base

    def copy(k):
        return pltpu.make_async_copy(
            weight.at[pl.ds(place(k)[0], fetched)], held.at[k, pl.ds(0, fetched)], sems.at[k]
        )

    for k in range(count):
        copy(k).start()
    lane = iota((blocks.shape[1], padded), 1)
    left, fill = scaled(), squares()

    def block(k, carry):
        copy(k).wait()
        product = dot_rows(left, held[k])
        moved = pltpu.roll(product, lax.rem(reach - place(k)[1], reach), 1)[:, :padded]
        blocks[k] = jnp.where(lane < share, moved, fill)
        return carry

    lax.fori_loop(0, count, block, 0, unroll=True)


def sems_rows(share):
    return -(-(share + 15) // 16) * 16


def other_kernel(share, parts, residual, gain, weight, blocks, scaled, squares, held, sems):
    def first():
        projected = sum(parts[k] for k in range(parts.shape[0]))
        stream = residual[...].astype(F32) + projected
        squares[...] = jnp.broadcast_to(
            jnp.sum(stream * stream, axis=1, keepdims=True), squares.shape
        )
        scaled[...] = (stream * gain[...]).astype(BF16)
        return scaled[...]

    head_blocks(True, share, first, lambda: squares[:, 0:1], weight, blocks, held, sems)


def same_kernel(share, scaled, squares, weight, blocks, held, sems):
    head_blocks(
        False, share, lambda: scaled[...], lambda: squares[:, 0:1], weight, blocks, held, sems
    )


def add_kernel(one, two, out):
    out[...] = one[...] + two[...]


def column_of(values, rows):
    shape = (rows, values.shape[1])
    return jnp.sum(jnp.where(iota(shape, 0) == iota(shape, 1), values, 0.0), axis=1, keepdims=True)


def stats_kernel(share, vocab, targets, parts, logits, spread):
    rows, padded = logits.shape
    summed = sum(parts[k] for k in range(parts.shape[0]))
    inverse = lax.rsqrt(summed[:, share : share + 1] * (1.0 / D) + NORM_EPS)
    lane = iota((rows, padded), 1)
    valid = lane < share
    local = summed * inverse
    logits[...] = local
    peak = jnp.max(jnp.where(valid, local, -jnp.inf), axis=1, keepdims=True)
    total = jnp.sum(jnp.where(valid, jnp.exp(local - peak), 0.0), axis=1, keepdims=True)
    row = iota((rows, 1), 0)
    wanted = jnp.zeros((rows, 1), jnp.int32)
    for b in range(rows // 2):
        wanted = jnp.where(lax.rem(row, rows // 2) == b, targets[b], wanted)
    start = lax.axis_index("tp") * vocab + lax.axis_index("ctx") * share
    hit = jnp.logical_and(valid, lane + start == wanted)
    picks = jnp.sum(jnp.where(hit, local, 0.0), axis=1, keepdims=True)
    place = iota((rows, 128), 1)
    mixed = jnp.where(place < rows, peak, jnp.where(place < 2 * rows, total, picks))
    keep = jnp.logical_and(lax.rem(place, rows) == iota((rows, 128), 0), place < 3 * rows)
    line = jnp.sum(jnp.where(keep, mixed, 0.0), axis=0, keepdims=True)
    spread[...] = jnp.broadcast_to(line, spread.shape)


def scores_kernel(share, everyone, logits, scores, chosen):
    rows = logits.shape[0]
    half = rows // 2
    data = everyone[...]
    peak = jnp.max(data, axis=0, keepdims=True)
    scale = jnp.exp(data - peak)
    lane = iota(peak.shape, 1)
    total = jnp.sum(pltpu.roll(scale, rows, 1) * data, axis=0, keepdims=True)
    total = jnp.where(lane < rows, pltpu.roll(total, 128 - rows, 1), 1.0)
    picks = pltpu.roll(jnp.sum(data, axis=0, keepdims=True), 128 - 2 * rows, 1)
    lse = peak + jnp.log(total)
    picked = picks - lse
    line = (
        (1.0 + CONTRAST_WEIGHT) * picked
        - CONTRAST_WEIGHT * pltpu.roll(picked, 128 - half, 1)
        + jnp.minimum(0.0, picks - peak - LOG_FLOOR)
    )
    chosen[...] = line[:, :half]
    logp = logits[...] - column_of(lse, rows)
    top = column_of(peak, rows)
    result = (
        (1.0 + CONTRAST_WEIGHT) * logp[:half]
        - CONTRAST_WEIGHT * logp[half:]
        + jnp.minimum(0.0, logits[:half] - top[:half] - LOG_FLOOR)
    )
    scores[...] = result[:, :share]


def call(kernel, out, in_specs, name, scratch=(), flops=0, moved=0):
    outs = [jax.ShapeDtypeStruct(shape, kind) for shape, kind in out]
    specs = [VMEM] * len(outs)
    return pl.pallas_call(
        kernel,
        out_shape=outs if len(outs) > 1 else outs[0],
        in_specs=in_specs,
        out_specs=specs if len(outs) > 1 else specs[0],
        scratch_shapes=list(scratch),
        name=name,
        cost_estimate=pl.CostEstimate(flops=flops, bytes_accessed=moved, transcendentals=0),
        compiler_params=pltpu.CompilerParams(vmem_limit_bytes=24 * 1024 * 1024),
    )


def per_device(
    queries,
    new_kv,
    long_cache,
    short_cache,
    lengths,
    residual,
    out_weight,
    final_gain,
    head_weight,
    targets,
):
    row_count, heads = queries.shape[1], queries.shape[2]
    block_len, short_len = long_cache.shape[2], short_cache.shape[2]
    width, vocab = residual.shape[2], head_weight.shape[1]
    ctx_size, tp_size = lax.axis_size("ctx"), lax.axis_size("tp")
    chips = ctx_size // 2
    rows = 2 * row_count
    share = vocab // ctx_size
    padded = -(-(share + 1) // 128) * 128
    pairs = row_count * heads
    packed = HEAD_DIM // 2 + 8
    cores = [(i, i ^ 1) for i in range(ctx_size)]
    same_core = [list(range(which, ctx_size, 2)) for which in range(2)]

    flat_queries = queries.reshape(2, pairs, HEAD_DIM)
    long_rows = long_cache.reshape(2, row_count, block_len, HEAD_DIM)
    short_rows = short_cache.reshape(2, row_count, short_len, HEAD_DIM)
    fresh = new_kv.reshape(2, 2, row_count, HEAD_DIM)

    chunks = 4
    state = call(
        functools.partial(long_kernel, chunks),
        [((packed, 128), F32)],
        [SMEM, VMEM, ANY],
        "long_attention",
        [
            pltpu.VMEM(long_rows.shape, BF16),
            pltpu.VMEM((pairs, HEAD_DIM), F32),
            pltpu.VMEM((pairs, HEAD_DIM), F32),
            pltpu.SemaphoreType.DMA((2 * chunks,)),
        ],
        moved=2 * 1024 * 1024,
    )(lengths, flat_queries, long_rows)
    other = lax.ppermute(state, "ctx", cores)
    aux = call(
        short_kernel, [((3, pairs, HEAD_DIM), F32)], [VMEM] * 3, "short_attention", moved=1024 * 1024
    )(flat_queries, short_rows, fresh)
    spread = call(pair_kernel, [((chips, packed, 128), F32)], [VMEM] * 2, "merge_cores")(
        state, other
    )
    states = lax.all_to_all(spread, "ctx", 0, 0, tiled=True, axis_index_groups=same_core)
    spread = call(project_kernel, [((tp_size, rows, width), F32)], [VMEM] * 3, "project")(
        states, aux, out_weight
    )
    parts = lax.all_to_all(spread, "tp", 0, 0, tiled=True)

    weight_rows = head_weight.T
    reach = -(-sems_rows(share) // 128) * 128
    scratch = [pltpu.VMEM((chips, reach, width), BF16), pltpu.SemaphoreType.DMA((chips,))]
    theirs, scaled, squares = call(
        functools.partial(other_kernel, share),
        [((chips, rows, padded), F32), ((rows, width), BF16), ((rows, 128), F32)],
        [VMEM, VMEM, VMEM, ANY],
        "head_other",
        scratch,
        moved=4 * 1024 * 1024,
    )(parts, residual.reshape(rows, width), final_gain.reshape(1, width), weight_rows)
    arrived = lax.ppermute(theirs, "ctx", cores)
    mine = call(
        functools.partial(same_kernel, share),
        [((chips, rows, padded), F32)],
        [VMEM, VMEM, ANY],
        "head_same",
        scratch,
        moved=4 * 1024 * 1024,
    )(scaled, squares, weight_rows)
    blocks = call(add_kernel, [((chips, rows, padded), F32)], [VMEM] * 2, "add_cores")(
        mine, arrived
    )
    parts = lax.all_to_all(blocks, "ctx", 0, 0, tiled=True, axis_index_groups=same_core)

    devices = ctx_size * tp_size
    logits, spread = call(
        functools.partial(stats_kernel, share, vocab),
        [((rows, padded), F32), ((devices, 128), F32)],
        [SMEM, VMEM],
        "vocab_stats",
    )(targets, parts)
    everyone = lax.all_to_all(
        spread.reshape(devices, 1, 128), ("ctx", "tp"), 0, 0, tiled=True
    ).reshape(devices, 128)
    scores, chosen = call(
        functools.partial(scores_kernel, share),
        [((row_count, share), F32), ((1, row_count), F32)],
        [VMEM, VMEM],
        "scores",
    )(everyone, logits)
    return (scores, chosen.reshape(row_count))


def solution(mesh):
    placed = (
        P(None, None, "tp", None),
        P(None, None, None, "tp", None),
        P(None, None, "ctx", "tp", None),
        P(None, None, None, "tp", None),
        P(),
        P(None, None, "ctx"),
        P("tp", "ctx"),
        P("ctx"),
        P("ctx", "tp"),
        P(),
    )
    return jax.shard_map(
        per_device,
        mesh=mesh,
        in_specs=placed,
        out_specs=(P(None, ("tp", "ctx")), P()),
        check_vma=False,
    )
```

```python
import functools

import jax
import jax.numpy as jnp
from jax import lax
from jax.experimental import pallas as pl
from jax.experimental.pallas import tpu as pltpu
from jax.sharding import PartitionSpec as P

D = 8192
HEAD_DIM = 128
SCORE_SCALE = HEAD_DIM ** (-0.5)

NEG_FILL = -1e30
NORM_EPS = 1e-05
CONTRAST_WEIGHT = 0.5
LOG_FLOOR = -2.302585092994046

F32 = jnp.float32
BF16 = jnp.bfloat16
VMEM = pl.BlockSpec(memory_space=pltpu.VMEM)
ANY = pl.BlockSpec(memory_space=pl.ANY)


def dot_rows(left, right):
    return lax.dot_general(left, right, (((1,), (1,)), ((), ())), preferred_element_type=F32)


def iota(shape, axis):
    return lax.broadcasted_iota(jnp.int32, shape, axis)


def long_kernel(
    chunks, lengths_far, queries_far, cache, state, held, queries, lengths, wide, stat, sems
):
    rows, block_len = cache.shape[1], cache.shape[2]
    per = rows // chunks
    small = [
        pltpu.make_async_copy(lengths_far, lengths, sems.at[2 * chunks]),
        pltpu.make_async_copy(queries_far.at[0], queries, sems.at[2 * chunks + 1]),
    ]
    for copy in small:
        copy.start()
    copies = [
        pltpu.make_async_copy(
            cache.at[part, pl.ds(c * per, per)],
            held.at[part, pl.ds(c * per, per)],
            sems.at[part * chunks + c],
        )
        for part in range(2)
        for c in range(chunks)
    ]
    for copy in copies:
        copy.start()
    start = lax.axis_index("ctx") * block_len
    for copy in small:
        copy.wait()
    query = queries[...].astype(F32)
    heads = query.shape[0] // rows
    position = start + iota((heads, block_len), 1)
    lane = iota((heads, HEAD_DIM), 1)
    kept = []
    for b in range(rows):
        if b % per == 0:
            copies[b // per].wait()
        mine = query[b * heads : (b + 1) * heads].astype(BF16)
        mask = position < lengths[b]
        scores = jnp.where(mask, dot_rows(mine, held[0, b]) * SCORE_SCALE, NEG_FILL)
        top = jnp.max(scores, axis=1, keepdims=True)
        weights = jnp.where(mask, jnp.exp(scores - top), 0.0)
        total = jnp.sum(weights, axis=1, keepdims=True)
        stat[pl.ds(b, heads, stride=rows), :] = jnp.where(lane == 0, top, total)
        kept.append(weights.astype(BF16))
    for b in range(rows):
        if b % per == 0:
            copies[chunks + b // per].wait()
        wide[pl.ds(b, heads, stride=rows), :] = jnp.dot(
            kept[b], held[1, b], preferred_element_type=F32
        )
    half = HEAD_DIM // 2
    turned = wide[...].T
    state[0:half, :] = jnp.concatenate([turned[:half], turned[half:]], axis=1)
    turned = stat[...].T[:8]
    state[half : half + 8, :] = jnp.concatenate([turned, turned], axis=1)


def short_kernel(
    share,
    queries_far,
    cache_far,
    fresh_far,
    out_far,
    head_far,
    residual_far,
    gain_far,
    targets_far,
    aux,
    out_near,
    head_near,
    residual,
    gain,
    wanted,
    queries,
    cache,
    fresh,
    targets,
    sems,
    head_sems,
):
    moves = (
        (queries_far, queries),
        (cache_far.at[0], cache.at[0]),
        (fresh_far, fresh),
        (cache_far.at[1], cache.at[1]),
        (targets_far, targets),
        (out_far, out_near),
        (residual_far, residual),
        (gain_far, gain),
    )
    copies = [pltpu.make_async_copy(*move, sems.at[n]) for n, move in enumerate(moves)]
    for copy in copies:
        copy.start()
    fetched = fetched_rows(share)
    blocks = [
        pltpu.make_async_copy(
            head_far.at[pl.ds(min(j * share // 16 * 16, head_far.shape[0] - fetched), fetched)],
            head_near.at[j, pl.ds(0, fetched)],
            head_sems.at[j],
        )
        for j in range(head_near.shape[0])
    ]
    for copy in blocks:
        copy.start()
    for copy in copies:
        copy.wait()
    row = iota(wanted.shape, 0)
    aim = jnp.zeros(wanted.shape, jnp.int32)
    for b in range(targets.shape[0]):
        aim = jnp.where(lax.rem(row, targets.shape[0]) == b, targets[b], aim)
    wanted[...] = aim
    rows = cache.shape[1]
    query = [queries[0].astype(F32), queries[1].astype(F32)]
    heads = query[0].shape[0] // rows
    key = [fresh[0, 0].astype(F32), fresh[1, 0].astype(F32)]
    value = [fresh[0, 1].astype(F32), fresh[1, 1].astype(F32)]
    for b in range(rows):
        part = [q[b * heads : (b + 1) * heads] for q in query]
        own = [
            jnp.sum(part[n] * key[n][b : b + 1], axis=1, keepdims=True) * SCORE_SCALE
            for n in range(2)
        ]
        scores = dot_rows(part[1].astype(BF16), cache[0, b]) * SCORE_SCALE
        top = jnp.max(scores, axis=1, keepdims=True)
        weights = jnp.exp(scores - top)
        total = jnp.sum(weights, axis=1, keepdims=True)
        output = jnp.dot(weights.astype(BF16), cache[1, b], preferred_element_type=F32)
        final = jnp.maximum(top, own[1])
        older = jnp.exp(top - final)
        newer = jnp.exp(own[1] - final)
        mixed = output * older + newer * value[1][b : b + 1]
        where = pl.ds(b, heads, stride=rows)
        aux[0, where, :] = mixed / (total * older + newer)
        aux[1, where, :] = jnp.broadcast_to(own[0], (heads, HEAD_DIM))
        aux[2, where, :] = jnp.broadcast_to(value[0][b : b + 1], (heads, HEAD_DIM))
    for copy in blocks:
        copy.wait()


def merge_states(parts):
    half = HEAD_DIM // 2
    tops = [part[half : half + 1, :] for part in parts]
    peak = functools.reduce(jnp.maximum, tops)
    factors = [jnp.exp(top - peak) for top in tops]
    total = sum(part[half + 1 : half + 2, :] * f for part, f in zip(parts, factors))
    values = sum(part[0:half, :] * f for part, f in zip(parts, factors))
    return values, peak, total


def packed_stats(peak, total):
    return jnp.where(iota((8, HEAD_DIM), 0) == 0, peak, total)


def pair_kernel(one, two, spread):
    half = HEAD_DIM // 2
    values, peak, total = merge_states([one, two])
    stats = packed_stats(peak, total)
    for k in range(spread.shape[0]):
        spread[k, 0:half, :] = values
        spread[k, half : half + 8, :] = stats


def project_kernel(states, aux, weight, spread):
    half = HEAD_DIM // 2
    values, peak, total = merge_states([states.at[k] for k in range(states.shape[0])])
    blank = jnp.zeros((half - 8, HEAD_DIM), F32)
    turned = jnp.concatenate([values, packed_stats(peak, total), blank], axis=0).T
    left, right = turned[:half], turned[half:]
    lane = iota((half, HEAD_DIM), 1)
    output = jnp.where(lane < half, left, pltpu.roll(right, half, 1))
    peak, total = left[:, half : half + 1], left[:, half + 1 : half + 2]
    own = aux[1][:, 0:1]
    final = jnp.maximum(peak, own)
    older = jnp.exp(peak - final)
    newer = jnp.exp(own - final)
    attended = [(output * older + newer * aux[2]) / (total * older + newer), aux[0]]
    rows = 8
    heads = half // rows
    rows_wide = jnp.concatenate(
        [
            jnp.concatenate([part[h * rows : (h + 1) * rows] for part in attended], axis=0)
            for h in range(heads)
        ],
        axis=1,
    )
    projected = jnp.dot(rows_wide.astype(BF16), weight[...], preferred_element_type=F32)
    for k in range(spread.shape[0]):
        spread[k] = projected


def fetched_rows(share):
    return -(-(share + 15) // 16) * 16


def head_blocks(other, share, vocab, left, fill, weight, blocks):
    padded, reach = blocks.shape[2], weight.shape[1]
    core = lax.rem(lax.axis_index("ctx"), 2)
    which = 1 - core if other else core
    lane = iota((blocks.shape[1], padded), 1)
    for k in range(blocks.shape[0]):
        j = 2 * k + which
        offset = j * share
        ahead = offset - jnp.minimum(offset // 16 * 16, vocab - fetched_rows(share))
        product = dot_rows(left, weight[j])
        moved = pltpu.roll(product, lax.rem(reach - ahead, reach), 1)[:, :padded]
        blocks[k] = jnp.where(lane < share, moved, fill)


def other_kernel(share, vocab, parts, residual, gain, weight, blocks, scaled, squares):
    projected = sum(parts[k] for k in range(parts.shape[0]))
    stream = residual[...].astype(F32) + projected
    fill = jnp.sum(stream * stream, axis=1, keepdims=True)
    squares[...] = jnp.broadcast_to(fill, squares.shape)
    left = (stream * gain[...]).astype(BF16)
    scaled[...] = left
    head_blocks(True, share, vocab, left, fill, weight, blocks)


def same_kernel(share, vocab, scaled, squares, weight, blocks):
    head_blocks(False, share, vocab, scaled[...], squares[:, 0:1], weight, blocks)


def add_kernel(one, two, out):
    out[...] = one[...] + two[...]


def column_of(values, rows):
    shape = (rows, values.shape[1])
    return jnp.sum(jnp.where(iota(shape, 0) == iota(shape, 1), values, 0.0), axis=1, keepdims=True)


def stats_kernel(share, vocab, wanted, parts, logits, spread):
    rows, padded = logits.shape
    summed = sum(parts[k] for k in range(parts.shape[0]))
    inverse = lax.rsqrt(summed[:, share : share + 1] * (1.0 / D) + NORM_EPS)
    lane = iota((rows, padded), 1)
    valid = lane < share
    local = summed * inverse
    logits[...] = local
    peak = jnp.max(jnp.where(valid, local, -jnp.inf), axis=1, keepdims=True)
    total = jnp.sum(jnp.where(valid, jnp.exp(local - peak), 0.0), axis=1, keepdims=True)
    start = lax.axis_index("tp") * vocab + lax.axis_index("ctx") * share
    hit = jnp.logical_and(valid, lane + start == wanted[:, 0:1])
    picks = jnp.sum(jnp.where(hit, local, 0.0), axis=1, keepdims=True)
    place = iota((rows, 128), 1)
    mixed = jnp.where(place < rows, peak, jnp.where(place < 2 * rows, total, picks))
    keep = jnp.logical_and(lax.rem(place, rows) == iota((rows, 128), 0), place < 3 * rows)
    line = jnp.sum(jnp.where(keep, mixed, 0.0), axis=0, keepdims=True)
    spread[...] = jnp.broadcast_to(line, spread.shape)


def scores_kernel(share, everyone, logits, scores, chosen):
    rows = logits.shape[0]
    half = rows // 2
    data = everyone[...]
    peak = jnp.max(data, axis=0, keepdims=True)
    scale = jnp.exp(data - peak)
    lane = iota(peak.shape, 1)
    total = jnp.sum(pltpu.roll(scale, rows, 1) * data, axis=0, keepdims=True)
    total = jnp.where(lane < rows, pltpu.roll(total, 128 - rows, 1), 1.0)
    picks = pltpu.roll(jnp.sum(data, axis=0, keepdims=True), 128 - 2 * rows, 1)
    lse = peak + jnp.log(total)
    picked = picks - lse
    line = (
        (1.0 + CONTRAST_WEIGHT) * picked
        - CONTRAST_WEIGHT * pltpu.roll(picked, 128 - half, 1)
        + jnp.minimum(0.0, picks - peak - LOG_FLOOR)
    )
    chosen[...] = line[:, :half]
    logp = logits[...] - column_of(lse, rows)
    top = column_of(peak, rows)
    result = (
        (1.0 + CONTRAST_WEIGHT) * logp[:half]
        - CONTRAST_WEIGHT * logp[half:]
        + jnp.minimum(0.0, logits[:half] - top[:half] - LOG_FLOOR)
    )
    scores[...] = result[:, :share]


def call(kernel, out, in_specs, name, scratch=(), flops=0, moved=0, near=pltpu.VMEM):
    outs = [near(shape, kind) for shape, kind in out]
    specs = [VMEM] * len(outs)
    run = pl.pallas_call(
        kernel,
        out_shape=outs if len(outs) > 1 else outs[0],
        in_specs=in_specs,
        out_specs=specs if len(outs) > 1 else specs[0],
        scratch_shapes=list(scratch),
        name=name,
        cost_estimate=pl.CostEstimate(flops=flops, bytes_accessed=moved, transcendentals=0),
        compiler_params=pltpu.CompilerParams(vmem_limit_bytes=16 * 1024 * 1024),
    )

    def pinned(*operands):
        return run(
            *(
                pltpu.with_memory_space_constraint(operand, pltpu.HBM) if spec is ANY else operand
                for operand, spec in zip(operands, in_specs)
            )
        )

    return pinned


def per_device(
    queries,
    new_kv,
    long_cache,
    short_cache,
    lengths,
    residual,
    out_weight,
    final_gain,
    head_weight,
    targets,
):
    row_count, heads = queries.shape[1], queries.shape[2]
    block_len, short_len = long_cache.shape[2], short_cache.shape[2]
    width, vocab = residual.shape[2], head_weight.shape[1]
    ctx_size, tp_size = lax.axis_size("ctx"), lax.axis_size("tp")
    chips = ctx_size // 2
    rows = 2 * row_count
    share = vocab // ctx_size
    padded = -(-(share + 1) // 128) * 128
    pairs = row_count * heads
    packed = HEAD_DIM // 2 + 8
    cores = [(i, i ^ 1) for i in range(ctx_size)]
    same_core = [list(range(which, ctx_size, 2)) for which in range(2)]

    flat_queries = queries.reshape(2, pairs, HEAD_DIM)
    long_rows = long_cache.reshape(2, row_count, block_len, HEAD_DIM)
    short_rows = short_cache.reshape(2, row_count, short_len, HEAD_DIM)
    fresh = new_kv.reshape(2, 2, row_count, HEAD_DIM)

    chunks = 4
    state = call(
        functools.partial(long_kernel, chunks),
        [((packed, 128), F32)],
        [ANY, ANY, ANY],
        "long_attention",
        [
            pltpu.VMEM(long_rows.shape, BF16),
            pltpu.VMEM((pairs, HEAD_DIM), BF16),
            pltpu.SMEM((row_count,), jnp.int32),
            pltpu.VMEM((pairs, HEAD_DIM), F32),
            pltpu.VMEM((pairs, HEAD_DIM), F32),
            pltpu.SemaphoreType.DMA((2 * chunks + 2,)),
        ],
        moved=2 * 1024 * 1024,
    )(lengths, flat_queries, long_rows)
    other = lax.ppermute(state, "ctx", cores)
    spread = call(pair_kernel, [((chips, packed, 128), F32)], [VMEM] * 2, "merge_cores")(
        state, other
    )
    spread, fresh = lax.optimization_barrier((spread, fresh))
    states = lax.all_to_all(spread, "ctx", 0, 0, tiled=True, axis_index_groups=same_core)
    reach = -(-fetched_rows(share) // 128) * 128
    aux, out_near, head_near, residual_near, gain_near, wanted = call(
        functools.partial(short_kernel, share),
        [
            ((3, pairs, HEAD_DIM), F32),
            (out_weight.shape, BF16),
            ((ctx_size, reach, width), BF16),
            ((rows, width), BF16),
            ((1, width), F32),
            ((rows, 128), jnp.int32),
        ],
        [ANY] * 8,
        "short_attention",
        [
            pltpu.VMEM(flat_queries.shape, BF16),
            pltpu.VMEM(short_rows.shape, BF16),
            pltpu.VMEM(fresh.shape, BF16),
            pltpu.SMEM((row_count,), jnp.int32),
            pltpu.SemaphoreType.DMA((8,)),
            pltpu.SemaphoreType.DMA((ctx_size,)),
        ],
        moved=10 * 1024 * 1024,
    )(
        flat_queries,
        short_rows,
        fresh,
        out_weight,
        head_weight.T,
        residual.reshape(rows, width),
        final_gain.reshape(1, width),
        targets,
    )
    spread = call(project_kernel, [((tp_size, rows, width), F32)], [VMEM] * 3, "project")(
        states, aux, out_near
    )
    parts = lax.all_to_all(spread, "tp", 0, 0, tiled=True)

    theirs, scaled, squares = call(
        functools.partial(other_kernel, share, vocab),
        [((chips, rows, padded), F32), ((rows, width), BF16), ((rows, 128), F32)],
        [VMEM] * 4,
        "head_other",
        moved=4 * 1024 * 1024,
    )(parts, residual_near, gain_near, head_near)
    arrived = lax.ppermute(theirs, "ctx", cores)
    mine = call(
        functools.partial(same_kernel, share, vocab),
        [((chips, rows, padded), F32)],
        [VMEM] * 3,
        "head_same",
        moved=4 * 1024 * 1024,
    )(scaled, squares, head_near)
    blocks = call(add_kernel, [((chips, rows, padded), F32)], [VMEM] * 2, "add_cores")(
        mine, arrived
    )
    parts = lax.all_to_all(blocks, "ctx", 0, 0, tiled=True, axis_index_groups=same_core)

    devices = ctx_size * tp_size
    logits, spread = call(
        functools.partial(stats_kernel, share, vocab),
        [((rows, padded), F32), ((devices, 128), F32)],
        [VMEM, VMEM],
        "vocab_stats",
    )(wanted, parts)
    everyone = lax.all_to_all(
        spread.reshape(devices, 1, 128), ("ctx", "tp"), 0, 0, tiled=True
    ).reshape(devices, 128)
    scores, chosen = call(
        functools.partial(scores_kernel, share),
        [((row_count, share), F32), ((1, row_count), F32)],
        [VMEM, VMEM],
        "scores",
        near=jax.ShapeDtypeStruct,
    )(everyone, logits)
    return (scores, chosen.reshape(row_count))


def solution(mesh):
    placed = (
        P(None, None, "tp", None),
        P(None, None, None, "tp", None),
        P(None, None, "ctx", "tp", None),
        P(None, None, None, "tp", None),
        P(),
        P(None, None, "ctx"),
        P("tp", "ctx"),
        P("ctx"),
        P("ctx", "tp"),
        P(),
    )
    return jax.shard_map(
        per_device,
        mesh=mesh,
        in_specs=placed,
        out_specs=(P(None, ("tp", "ctx")), P()),
        check_vma=False,
    )
```

```python
import functools

import jax
import jax.numpy as jnp
from jax import lax
from jax.experimental import pallas as pl
from jax.experimental.pallas import tpu as pltpu
from jax.sharding import PartitionSpec as P

D = 8192
HEAD_DIM = 128
SCORE_SCALE = HEAD_DIM ** (-0.5)

NEG_FILL = -1e30
NORM_EPS = 1e-05
CONTRAST_WEIGHT = 0.5
LOG_FLOOR = -2.302585092994046

F32 = jnp.float32
BF16 = jnp.bfloat16
VMEM = pl.BlockSpec(memory_space=pltpu.VMEM)
ANY = pl.BlockSpec(memory_space=pl.ANY)


def dot_rows(left, right):
    return lax.dot_general(left, right, (((1,), (1,)), ((), ())), preferred_element_type=F32)


def iota(shape, axis):
    return lax.broadcasted_iota(jnp.int32, shape, axis)


def long_kernel(
    chunks, lengths_far, queries_far, cache, state, held, queries, lengths, wide, stat, sems
):
    rows, block_len = cache.shape[1], cache.shape[2]
    per = rows // chunks
    small = [
        pltpu.make_async_copy(lengths_far, lengths, sems.at[2 * chunks]),
        pltpu.make_async_copy(queries_far.at[0], queries, sems.at[2 * chunks + 1]),
    ]
    for copy in small:
        copy.start()
    copies = [
        pltpu.make_async_copy(
            cache.at[part, pl.ds(c * per, per)],
            held.at[part, pl.ds(c * per, per)],
            sems.at[part * chunks + c],
        )
        for part in range(2)
        for c in range(chunks)
    ]
    for copy in copies:
        copy.start()
    start = lax.axis_index("ctx") * block_len
    for copy in small:
        copy.wait()
    query = queries[...].astype(F32)
    heads = query.shape[0] // rows
    position = start + iota((heads, block_len), 1)
    lane = iota((heads, HEAD_DIM), 1)
    kept = []
    for b in range(rows):
        if b % per == 0:
            copies[b // per].wait()
        mine = query[b * heads : (b + 1) * heads].astype(BF16)
        mask = position < lengths[b]
        scores = jnp.where(mask, dot_rows(mine, held[0, b]) * SCORE_SCALE, NEG_FILL)
        top = jnp.max(scores, axis=1, keepdims=True)
        weights = jnp.where(mask, jnp.exp(scores - top), 0.0)
        total = jnp.sum(weights, axis=1, keepdims=True)
        stat[pl.ds(b, heads, stride=rows), :] = jnp.where(lane == 0, top, total)
        kept.append(weights.astype(BF16))
    for b in range(rows):
        if b % per == 0:
            copies[chunks + b // per].wait()
        wide[pl.ds(b, heads, stride=rows), :] = jnp.dot(
            kept[b], held[1, b], preferred_element_type=F32
        )
    half = HEAD_DIM // 2
    turned = wide[...].T
    state[0:half, :] = jnp.concatenate([turned[:half], turned[half:]], axis=1)
    turned = stat[...].T[:8]
    state[half : half + 8, :] = jnp.concatenate([turned, turned], axis=1)


def short_kernel(
    queries_far,
    cache_far,
    fresh_far,
    out_far,
    residual_far,
    gain_far,
    targets_far,
    aux,
    out_near,
    residual,
    gain,
    wanted,
    queries,
    cache,
    fresh,
    targets,
    sems,
):
    moves = (
        (queries_far, queries),
        (cache_far.at[0], cache.at[0]),
        (fresh_far, fresh),
        (cache_far.at[1], cache.at[1]),
        (targets_far, targets),
        (out_far, out_near),
        (residual_far, residual),
        (gain_far, gain),
    )
    copies = [pltpu.make_async_copy(*move, sems.at[n]) for n, move in enumerate(moves)]
    for copy in copies:
        copy.start()
    for copy in copies:
        copy.wait()
    row = iota(wanted.shape, 0)
    aim = jnp.zeros(wanted.shape, jnp.int32)
    for b in range(targets.shape[0]):
        aim = jnp.where(lax.rem(row, targets.shape[0]) == b, targets[b], aim)
    wanted[...] = aim
    rows = cache.shape[1]
    query = [queries[0].astype(F32), queries[1].astype(F32)]
    heads = query[0].shape[0] // rows
    key = [fresh[0, 0].astype(F32), fresh[1, 0].astype(F32)]
    value = [fresh[0, 1].astype(F32), fresh[1, 1].astype(F32)]
    for b in range(rows):
        part = [q[b * heads : (b + 1) * heads] for q in query]
        own = [
            jnp.sum(part[n] * key[n][b : b + 1], axis=1, keepdims=True) * SCORE_SCALE
            for n in range(2)
        ]
        scores = dot_rows(part[1].astype(BF16), cache[0, b]) * SCORE_SCALE
        top = jnp.max(scores, axis=1, keepdims=True)
        weights = jnp.exp(scores - top)
        total = jnp.sum(weights, axis=1, keepdims=True)
        output = jnp.dot(weights.astype(BF16), cache[1, b], preferred_element_type=F32)
        final = jnp.maximum(top, own[1])
        older = jnp.exp(top - final)
        newer = jnp.exp(own[1] - final)
        mixed = output * older + newer * value[1][b : b + 1]
        where = pl.ds(b, heads, stride=rows)
        aux[0, where, :] = mixed / (total * older + newer)
        aux[1, where, :] = jnp.broadcast_to(own[0], (heads, HEAD_DIM))
        aux[2, where, :] = jnp.broadcast_to(value[0][b : b + 1], (heads, HEAD_DIM))


def merge_states(parts):
    half = HEAD_DIM // 2
    tops = [part[half : half + 1, :] for part in parts]
    peak = functools.reduce(jnp.maximum, tops)
    factors = [jnp.exp(top - peak) for top in tops]
    total = sum(part[half + 1 : half + 2, :] * f for part, f in zip(parts, factors))
    values = sum(part[0:half, :] * f for part, f in zip(parts, factors))
    return values, peak, total


def packed_stats(peak, total):
    return jnp.where(iota((8, HEAD_DIM), 0) == 0, peak, total)


def pair_kernel(one, two, spread):
    half = HEAD_DIM // 2
    values, peak, total = merge_states([one, two])
    stats = packed_stats(peak, total)
    for k in range(spread.shape[0]):
        spread[k, 0:half, :] = values
        spread[k, half : half + 8, :] = stats


def project_kernel(states, aux, weight, spread):
    half = HEAD_DIM // 2
    values, peak, total = merge_states([states.at[k] for k in range(states.shape[0])])
    blank = jnp.zeros((half - 8, HEAD_DIM), F32)
    turned = jnp.concatenate([values, packed_stats(peak, total), blank], axis=0).T
    left, right = turned[:half], turned[half:]
    lane = iota((half, HEAD_DIM), 1)
    output = jnp.where(lane < half, left, pltpu.roll(right, half, 1))
    peak, total = left[:, half : half + 1], left[:, half + 1 : half + 2]
    own = aux[1][:, 0:1]
    final = jnp.maximum(peak, own)
    older = jnp.exp(peak - final)
    newer = jnp.exp(own - final)
    attended = [(output * older + newer * aux[2]) / (total * older + newer), aux[0]]
    rows = 8
    heads = half // rows
    rows_wide = jnp.concatenate(
        [
            jnp.concatenate([part[h * rows : (h + 1) * rows] for part in attended], axis=0)
            for h in range(heads)
        ],
        axis=1,
    )
    projected = jnp.dot(rows_wide.astype(BF16), weight[...], preferred_element_type=F32)
    for k in range(spread.shape[0]):
        spread[k] = projected


def fetched_rows(share):
    return -(-(share + 15) // 16) * 16


def block_start(j, share, vocab):
    return jnp.minimum(j * share // 16 * 16, vocab - fetched_rows(share))


def head_block(k, which, share, vocab, left, fill, weight, blocks):
    padded, reach = blocks.shape[2], weight.shape[1]
    j = 2 * k + which
    ahead = j * share - block_start(j, share, vocab)
    product = dot_rows(left, weight[k])
    moved = pltpu.roll(product, lax.rem(reach - ahead, reach), 1)[:, :padded]
    lane = iota(moved.shape, 1)
    blocks[k] = jnp.where(lane < share, moved, fill)


def other_kernel(
    share, group, parts, residual, gain, weight, blocks, scaled, squares, kept, held, sems
):
    vocab, count = weight.shape[0], blocks.shape[0]
    fetched = fetched_rows(share)
    core = lax.rem(lax.axis_index("ctx"), 2)

    def copy(k, which, place, sem):
        base = pl.multiple_of(block_start(2 * k + which, share, vocab), 16)
        return pltpu.make_async_copy(
            weight.at[pl.ds(base, fetched)], place.at[k, pl.ds(0, fetched)], sem
        )

    first = [copy(k, 1 - core, held, sems.at[k]) for k in range(count)]
    second = [copy(k, core, kept, sems.at[count + k]) for k in range(count)]
    for one in first + second:
        one.start()
    projected = sum(parts[k] for k in range(parts.shape[0]))
    stream = residual[...].astype(F32) + projected
    fill = jnp.sum(stream * stream, axis=1, keepdims=True)
    squares[...] = jnp.broadcast_to(fill, squares.shape)
    left = (stream * gain[...]).astype(BF16)
    scaled[...] = left
    for start in range(0, count, group):
        for one in first[start : start + group]:
            one.wait()
        for k in range(start, start + group):
            head_block(k, 1 - core, share, vocab, left, fill, held, blocks)
    for one in second:
        one.wait()


def same_kernel(share, vocab, scaled, squares, weight, blocks):
    core = lax.rem(lax.axis_index("ctx"), 2)
    for k in range(blocks.shape[0]):
        head_block(k, core, share, vocab, scaled[...], squares[:, 0:1], weight, blocks)


def add_kernel(one, two, out):
    out[...] = one[...] + two[...]


def column_of(values, rows):
    shape = (rows, values.shape[1])
    return jnp.sum(jnp.where(iota(shape, 0) == iota(shape, 1), values, 0.0), axis=1, keepdims=True)


def stats_kernel(share, vocab, wanted, parts, logits, spread):
    rows, padded = logits.shape
    summed = sum(parts[k] for k in range(parts.shape[0]))
    inverse = lax.rsqrt(summed[:, share : share + 1] * (1.0 / D) + NORM_EPS)
    lane = iota((rows, padded), 1)
    valid = lane < share
    local = summed * inverse
    logits[...] = local
    peak = jnp.max(jnp.where(valid, local, -jnp.inf), axis=1, keepdims=True)
    total = jnp.sum(jnp.where(valid, jnp.exp(local - peak), 0.0), axis=1, keepdims=True)
    start = lax.axis_index("tp") * vocab + lax.axis_index("ctx") * share
    hit = jnp.logical_and(valid, lane + start == wanted[:, 0:1])
    picks = jnp.sum(jnp.where(hit, local, 0.0), axis=1, keepdims=True)
    place = iota((rows, 128), 1)
    mixed = jnp.where(place < rows, peak, jnp.where(place < 2 * rows, total, picks))
    keep = jnp.logical_and(lax.rem(place, rows) == iota((rows, 128), 0), place < 3 * rows)
    line = jnp.sum(jnp.where(keep, mixed, 0.0), axis=0, keepdims=True)
    spread[...] = jnp.broadcast_to(line, spread.shape)


def scores_kernel(share, everyone, logits, scores, chosen):
    rows = logits.shape[0]
    half = rows // 2
    data = everyone[...]
    peak = jnp.max(data, axis=0, keepdims=True)
    scale = jnp.exp(data - peak)
    lane = iota(peak.shape, 1)
    total = jnp.sum(pltpu.roll(scale, rows, 1) * data, axis=0, keepdims=True)
    total = jnp.where(lane < rows, pltpu.roll(total, 128 - rows, 1), 1.0)
    picks = pltpu.roll(jnp.sum(data, axis=0, keepdims=True), 128 - 2 * rows, 1)
    lse = peak + jnp.log(total)
    picked = picks - lse
    line = (
        (1.0 + CONTRAST_WEIGHT) * picked
        - CONTRAST_WEIGHT * pltpu.roll(picked, 128 - half, 1)
        + jnp.minimum(0.0, picks - peak - LOG_FLOOR)
    )
    chosen[...] = line[:, :half]
    logp = logits[...] - column_of(lse, rows)
    top = column_of(peak, rows)
    result = (
        (1.0 + CONTRAST_WEIGHT) * logp[:half]
        - CONTRAST_WEIGHT * logp[half:]
        + jnp.minimum(0.0, logits[:half] - top[:half] - LOG_FLOOR)
    )
    scores[...] = result[:, :share]


def call(kernel, out, in_specs, name, scratch=(), flops=0, moved=0, near=pltpu.VMEM):
    outs = [near(shape, kind) for shape, kind in out]
    specs = [VMEM] * len(outs)
    run = pl.pallas_call(
        kernel,
        out_shape=outs if len(outs) > 1 else outs[0],
        in_specs=in_specs,
        out_specs=specs if len(outs) > 1 else specs[0],
        scratch_shapes=list(scratch),
        name=name,
        cost_estimate=pl.CostEstimate(flops=flops, bytes_accessed=moved, transcendentals=0),
        compiler_params=pltpu.CompilerParams(vmem_limit_bytes=16 * 1024 * 1024),
    )

    def pinned(*operands):
        return run(
            *(
                pltpu.with_memory_space_constraint(operand, pltpu.HBM) if spec is ANY else operand
                for operand, spec in zip(operands, in_specs)
            )
        )

    return pinned


def per_device(
    queries,
    new_kv,
    long_cache,
    short_cache,
    lengths,
    residual,
    out_weight,
    final_gain,
    head_weight,
    targets,
):
    row_count, heads = queries.shape[1], queries.shape[2]
    block_len, short_len = long_cache.shape[2], short_cache.shape[2]
    width, vocab = residual.shape[2], head_weight.shape[1]
    ctx_size, tp_size = lax.axis_size("ctx"), lax.axis_size("tp")
    chips = ctx_size // 2
    rows = 2 * row_count
    share = vocab // ctx_size
    padded = -(-(share + 1) // 128) * 128
    pairs = row_count * heads
    packed = HEAD_DIM // 2 + 8
    cores = [(i, i ^ 1) for i in range(ctx_size)]
    same_core = [list(range(which, ctx_size, 2)) for which in range(2)]

    flat_queries = queries.reshape(2, pairs, HEAD_DIM)
    long_rows = long_cache.reshape(2, row_count, block_len, HEAD_DIM)
    short_rows = short_cache.reshape(2, row_count, short_len, HEAD_DIM)
    fresh = new_kv.reshape(2, 2, row_count, HEAD_DIM)

    chunks = 4
    state = call(
        functools.partial(long_kernel, chunks),
        [((packed, 128), F32)],
        [ANY, ANY, ANY],
        "long_attention",
        [
            pltpu.VMEM(long_rows.shape, BF16),
            pltpu.VMEM((pairs, HEAD_DIM), BF16),
            pltpu.SMEM((row_count,), jnp.int32),
            pltpu.VMEM((pairs, HEAD_DIM), F32),
            pltpu.VMEM((pairs, HEAD_DIM), F32),
            pltpu.SemaphoreType.DMA((2 * chunks + 2,)),
        ],
        moved=2 * 1024 * 1024,
    )(lengths, flat_queries, long_rows)
    other = lax.ppermute(state, "ctx", cores)
    spread = call(pair_kernel, [((chips, packed, 128), F32)], [VMEM] * 2, "merge_cores")(
        state, other
    )
    spread, fresh = lax.optimization_barrier((spread, fresh))
    states = lax.all_to_all(spread, "ctx", 0, 0, tiled=True, axis_index_groups=same_core)
    aux, out_near, residual_near, gain_near, wanted = call(
        short_kernel,
        [
            ((3, pairs, HEAD_DIM), F32),
            (out_weight.shape, BF16),
            ((rows, width), BF16),
            ((1, width), F32),
            ((rows, 128), jnp.int32),
        ],
        [ANY] * 7,
        "short_attention",
        [
            pltpu.VMEM(flat_queries.shape, BF16),
            pltpu.VMEM(short_rows.shape, BF16),
            pltpu.VMEM(fresh.shape, BF16),
            pltpu.SMEM((row_count,), jnp.int32),
            pltpu.SemaphoreType.DMA((8,)),
        ],
        moved=2 * 1024 * 1024,
    )(
        flat_queries,
        short_rows,
        fresh,
        out_weight,
        residual.reshape(rows, width),
        final_gain.reshape(1, width),
        targets,
    )
    spread = call(project_kernel, [((tp_size, rows, width), F32)], [VMEM] * 3, "project")(
        states, aux, out_near
    )
    parts = lax.all_to_all(spread, "tp", 0, 0, tiled=True)

    reach = -(-fetched_rows(share) // 128) * 128
    theirs, scaled, squares, head_near = call(
        functools.partial(other_kernel, share, chips // 4),
        [
            ((chips, rows, padded), F32),
            ((rows, width), BF16),
            ((rows, 128), F32),
            ((chips, reach, width), BF16),
        ],
        [VMEM, VMEM, VMEM, ANY],
        "head_other",
        [
            pltpu.VMEM((chips, reach, width), BF16),
            pltpu.SemaphoreType.DMA((2 * chips,)),
        ],
        moved=8 * 1024 * 1024,
    )(parts, residual_near, gain_near, head_weight.T)
    arrived = lax.ppermute(theirs, "ctx", cores)
    mine = call(
        functools.partial(same_kernel, share, vocab),
        [((chips, rows, padded), F32)],
        [VMEM] * 3,
        "head_same",
        moved=4 * 1024 * 1024,
    )(scaled, squares, head_near)
    blocks = call(add_kernel, [((chips, rows, padded), F32)], [VMEM] * 2, "add_cores")(
        mine, arrived
    )
    parts = lax.all_to_all(blocks, "ctx", 0, 0, tiled=True, axis_index_groups=same_core)

    devices = ctx_size * tp_size
    logits, spread = call(
        functools.partial(stats_kernel, share, vocab),
        [((rows, padded), F32), ((devices, 128), F32)],
        [VMEM, VMEM],
        "vocab_stats",
    )(wanted, parts)
    everyone = lax.all_to_all(
        spread.reshape(devices, 1, 128), ("ctx", "tp"), 0, 0, tiled=True
    ).reshape(devices, 128)
    scores, chosen = call(
        functools.partial(scores_kernel, share),
        [((row_count, share), F32), ((1, row_count), F32)],
        [VMEM, VMEM],
        "scores",
        near=jax.ShapeDtypeStruct,
    )(everyone, logits)
    return (scores, chosen.reshape(row_count))


def solution(mesh):
    placed = (
        P(None, None, "tp", None),
        P(None, None, None, "tp", None),
        P(None, None, "ctx", "tp", None),
        P(None, None, None, "tp", None),
        P(),
        P(None, None, "ctx"),
        P("tp", "ctx"),
        P("ctx"),
        P("ctx", "tp"),
        P(),
    )
    return jax.shard_map(
        per_device,
        mesh=mesh,
        in_specs=placed,
        out_specs=(P(None, ("tp", "ctx")), P()),
        check_vma=False,
    )
```

```python
import functools

import jax
import jax.numpy as jnp
from jax import lax
from jax.experimental import pallas as pl
from jax.experimental.pallas import tpu as pltpu
from jax.sharding import PartitionSpec as P

D = 8192
HEAD_DIM = 128
SCORE_SCALE = HEAD_DIM ** (-0.5)

NEG_FILL = -1e30
NORM_EPS = 1e-05
CONTRAST_WEIGHT = 0.5
LOG_FLOOR = -2.302585092994046

F32 = jnp.float32
BF16 = jnp.bfloat16
VMEM = pl.BlockSpec(memory_space=pltpu.VMEM)
ANY = pl.BlockSpec(memory_space=pl.ANY)


def dot_rows(left, right):
    return lax.dot_general(left, right, (((1,), (1,)), ((), ())), preferred_element_type=F32)


def iota(shape, axis):
    return lax.broadcasted_iota(jnp.int32, shape, axis)


def finish(copies):
    @pl.when(lax.axis_index("ctx") >= 0)
    def _():
        for copy in copies:
            copy.wait()


def attention_kernel(
    pieces,
    lengths_far,
    queries_far,
    long_far,
    short_far,
    fresh_far,
    targets_far,
    residual_far,
    gain_far,
    out_far,
    head_far,
    state,
    aux,
    wanted,
    residual,
    gain,
    out_near,
    head_near,
    lengths,
    targets,
    queries,
    fresh,
    long_near,
    short_near,
    wide,
    stat,
    sems,
):
    step = head_far.shape[0] // pieces // 16 * 16
    cuts = [step * n for n in range(pieces)] + [head_far.shape[0]]
    moves = [
        (lengths_far, lengths),
        (queries_far, queries),
        (long_far.at[0], long_near.at[0]),
        (fresh_far, fresh),
        (short_far.at[0], short_near.at[0]),
        (long_far.at[1], long_near.at[1]),
        (short_far.at[1], short_near.at[1]),
        (targets_far, targets),
        (residual_far, residual),
        (gain_far, gain),
        (out_far, out_near),
    ] + [
        (head_far.at[pl.ds(low, high - low)], head_near.at[pl.ds(low, high - low)])
        for low, high in zip(cuts, cuts[1:])
    ]
    copies = [pltpu.make_async_copy(*move, sems.at[n]) for n, move in enumerate(moves)]
    for copy in copies:
        copy.start()
    rows, block_len = long_far.shape[1], long_far.shape[2]
    finish(copies[:5])
    query = [queries[0].astype(F32), queries[1].astype(F32)]
    heads = query[0].shape[0] // rows
    key = [fresh[0, 0].astype(F32), fresh[1, 0].astype(F32)]
    value = [fresh[0, 1].astype(F32), fresh[1, 1].astype(F32)]
    position = lax.axis_index("ctx") * block_len + iota((heads, block_len), 1)
    lane = iota((heads, HEAD_DIM), 1)
    kept, kept_short = [], []
    for b in range(rows):
        part = [q[b * heads : (b + 1) * heads] for q in query]
        mask = position < lengths[b]
        scores = dot_rows(part[0].astype(BF16), long_near[0, b]) * SCORE_SCALE
        scores = jnp.where(mask, scores, NEG_FILL)
        top = jnp.max(scores, axis=1, keepdims=True)
        weights = jnp.where(mask, jnp.exp(scores - top), 0.0)
        total = jnp.sum(weights, axis=1, keepdims=True)
        stat[pl.ds(b, heads, stride=rows), :] = jnp.where(lane == 0, top, total)
        kept.append(weights.astype(BF16))
        own = [
            jnp.sum(part[n] * key[n][b : b + 1], axis=1, keepdims=True) * SCORE_SCALE
            for n in range(2)
        ]
        scores = dot_rows(part[1].astype(BF16), short_near[0, b]) * SCORE_SCALE
        top = jnp.max(scores, axis=1, keepdims=True)
        weights = jnp.exp(scores - top)
        final = jnp.maximum(top, own[1])
        older = jnp.exp(top - final)
        newer = jnp.exp(own[1] - final)
        scale = 1.0 / (jnp.sum(weights, axis=1, keepdims=True) * older + newer)
        kept_short.append((weights.astype(BF16), older * scale, newer * scale))
        where = pl.ds(b, heads, stride=rows)
        aux[1, where, :] = jnp.broadcast_to(own[0], (heads, HEAD_DIM))
        aux[2, where, :] = jnp.broadcast_to(value[0][b : b + 1], (heads, HEAD_DIM))
    finish(copies[5:8])
    for b in range(rows):
        where = pl.ds(b, heads, stride=rows)
        wide[where, :] = jnp.dot(kept[b], long_near[1, b], preferred_element_type=F32)
        weights, older, newer = kept_short[b]
        output = jnp.dot(weights, short_near[1, b], preferred_element_type=F32)
        aux[0, where, :] = output * older + newer * value[1][b : b + 1]
    half = HEAD_DIM // 2
    turned = wide[...].T
    state[0:half, :] = jnp.concatenate([turned[:half], turned[half:]], axis=1)
    turned = stat[...].T[:8]
    state[half : half + 8, :] = jnp.concatenate([turned, turned], axis=1)
    row = iota(wanted.shape, 0)
    aim = jnp.zeros(wanted.shape, jnp.int32)
    for b in range(rows):
        aim = jnp.where(lax.rem(row, rows) == b, targets[b], aim)
    wanted[...] = aim
    finish(copies[8:])


def merge_states(parts):
    half = HEAD_DIM // 2
    tops = [part[half : half + 1, :] for part in parts]
    peak = functools.reduce(jnp.maximum, tops)
    factors = [jnp.exp(top - peak) for top in tops]
    total = sum(part[half + 1 : half + 2, :] * f for part, f in zip(parts, factors))
    values = sum(part[0:half, :] * f for part, f in zip(parts, factors))
    return values, peak, total


def packed_stats(peak, total):
    return jnp.where(iota((8, HEAD_DIM), 0) == 0, peak, total)


def pair_kernel(one, two, spread):
    half = HEAD_DIM // 2
    values, peak, total = merge_states([one, two])
    stats = packed_stats(peak, total)
    for k in range(spread.shape[0]):
        spread[k, 0:half, :] = values
        spread[k, half : half + 8, :] = stats


def project_kernel(states, aux, weight, spread):
    half = HEAD_DIM // 2
    values, peak, total = merge_states([states.at[k] for k in range(states.shape[0])])
    blank = jnp.zeros((half - 8, HEAD_DIM), F32)
    turned = jnp.concatenate([values, packed_stats(peak, total), blank], axis=0).T
    left, right = turned[:half], turned[half:]
    lane = iota((half, HEAD_DIM), 1)
    output = jnp.where(lane < half, left, pltpu.roll(right, half, 1))
    peak, total = left[:, half : half + 1], left[:, half + 1 : half + 2]
    own = aux[1][:, 0:1]
    final = jnp.maximum(peak, own)
    older = jnp.exp(peak - final)
    newer = jnp.exp(own - final)
    attended = [(output * older + newer * aux[2]) / (total * older + newer), aux[0]]
    rows = 8
    heads = half // rows
    rows_wide = jnp.concatenate(
        [
            jnp.concatenate([part[h * rows : (h + 1) * rows] for part in attended], axis=0)
            for h in range(heads)
        ],
        axis=1,
    )
    projected = jnp.dot(rows_wide.astype(BF16), weight[...], preferred_element_type=F32)
    for k in range(spread.shape[0]):
        spread[k] = projected


def head_blocks(other, share, left, fill, weight, blocks):
    vocab, padded = weight.shape[0], blocks.shape[2]
    reach = -(-(share + 15) // 128) * 128
    core = lax.rem(lax.axis_index("ctx"), 2)
    which = 1 - core if other else core
    lane = iota((blocks.shape[1], padded), 1)
    for k in range(blocks.shape[0]):
        offset = (2 * k + which) * share
        base = pl.multiple_of(jnp.minimum(offset // 16 * 16, vocab - reach), 16)
        product = dot_rows(left, weight[pl.ds(base, reach), :])
        moved = pltpu.roll(product, lax.rem(reach - (offset - base), reach), 1)[:, :padded]
        blocks[k] = jnp.where(lane < share, moved, fill)


def other_kernel(share, parts, residual, gain, weight, blocks, scaled, squares):
    projected = sum(parts[k] for k in range(parts.shape[0]))
    stream = residual[...].astype(F32) + projected
    fill = jnp.sum(stream * stream, axis=1, keepdims=True)
    squares[...] = jnp.broadcast_to(fill, squares.shape)
    left = (stream * gain[...]).astype(BF16)
    scaled[...] = left
    head_blocks(True, share, left, fill, weight, blocks)


def same_kernel(share, scaled, squares, weight, blocks):
    head_blocks(False, share, scaled[...], squares[:, 0:1], weight, blocks)


def add_kernel(one, two, out):
    out[...] = one[...] + two[...]


def column_of(values, rows):
    shape = (rows, values.shape[1])
    return jnp.sum(jnp.where(iota(shape, 0) == iota(shape, 1), values, 0.0), axis=1, keepdims=True)


def stats_kernel(share, vocab, wanted, parts, logits, spread):
    rows, padded = logits.shape
    summed = sum(parts[k] for k in range(parts.shape[0]))
    inverse = lax.rsqrt(summed[:, share : share + 1] * (1.0 / D) + NORM_EPS)
    lane = iota((rows, padded), 1)
    valid = lane < share
    local = summed * inverse
    logits[...] = local
    peak = jnp.max(jnp.where(valid, local, -jnp.inf), axis=1, keepdims=True)
    total = jnp.sum(jnp.where(valid, jnp.exp(local - peak), 0.0), axis=1, keepdims=True)
    start = lax.axis_index("tp") * vocab + lax.axis_index("ctx") * share
    hit = jnp.logical_and(valid, lane + start == wanted[:, 0:1])
    picks = jnp.sum(jnp.where(hit, local, 0.0), axis=1, keepdims=True)
    place = iota((rows, 128), 1)
    mixed = jnp.where(place < rows, peak, jnp.where(place < 2 * rows, total, picks))
    keep = jnp.logical_and(lax.rem(place, rows) == iota((rows, 128), 0), place < 3 * rows)
    line = jnp.sum(jnp.where(keep, mixed, 0.0), axis=0, keepdims=True)
    spread[...] = jnp.broadcast_to(line, spread.shape)


def scores_kernel(share, everyone, logits, scores, chosen):
    rows = logits.shape[0]
    half = rows // 2
    data = everyone[...]
    peak = jnp.max(data, axis=0, keepdims=True)
    scale = jnp.exp(data - peak)
    lane = iota(peak.shape, 1)
    total = jnp.sum(pltpu.roll(scale, rows, 1) * data, axis=0, keepdims=True)
    total = jnp.where(lane < rows, pltpu.roll(total, 128 - rows, 1), 1.0)
    picks = pltpu.roll(jnp.sum(data, axis=0, keepdims=True), 128 - 2 * rows, 1)
    lse = peak + jnp.log(total)
    picked = picks - lse
    line = (
        (1.0 + CONTRAST_WEIGHT) * picked
        - CONTRAST_WEIGHT * pltpu.roll(picked, 128 - half, 1)
        + jnp.minimum(0.0, picks - peak - LOG_FLOOR)
    )
    chosen[...] = line[:, :half]
    logp = logits[...] - column_of(lse, rows)
    top = column_of(peak, rows)
    result = (
        (1.0 + CONTRAST_WEIGHT) * logp[:half]
        - CONTRAST_WEIGHT * logp[half:]
        + jnp.minimum(0.0, logits[:half] - top[:half] - LOG_FLOOR)
    )
    scores[...] = result[:, :share]


def call(kernel, out, in_specs, name, scratch=(), flops=0, moved=0, near=pltpu.VMEM):
    outs = [near(shape, kind) for shape, kind in out]
    specs = [VMEM] * len(outs)
    run = pl.pallas_call(
        kernel,
        out_shape=outs if len(outs) > 1 else outs[0],
        in_specs=in_specs,
        out_specs=specs if len(outs) > 1 else specs[0],
        scratch_shapes=list(scratch),
        name=name,
        cost_estimate=pl.CostEstimate(flops=flops, bytes_accessed=moved, transcendentals=0),
        compiler_params=pltpu.CompilerParams(vmem_limit_bytes=16 * 1024 * 1024),
    )

    def pinned(*operands):
        return run(
            *(
                pltpu.with_memory_space_constraint(operand, pltpu.HBM) if spec is ANY else operand
                for operand, spec in zip(operands, in_specs)
            )
        )

    return pinned


def per_device(
    queries,
    new_kv,
    long_cache,
    short_cache,
    lengths,
    residual,
    out_weight,
    final_gain,
    head_weight,
    targets,
):
    row_count, heads = queries.shape[1], queries.shape[2]
    block_len, short_len = long_cache.shape[2], short_cache.shape[2]
    width, vocab = residual.shape[2], head_weight.shape[1]
    ctx_size, tp_size = lax.axis_size("ctx"), lax.axis_size("tp")
    chips = ctx_size // 2
    rows = 2 * row_count
    share = vocab // ctx_size
    padded = -(-(share + 1) // 128) * 128
    pairs = row_count * heads
    packed = HEAD_DIM // 2 + 8
    cores = [(i, i ^ 1) for i in range(ctx_size)]
    same_core = [list(range(which, ctx_size, 2)) for which in range(2)]

    flat_queries = queries.reshape(2, pairs, HEAD_DIM)
    long_rows = long_cache.reshape(2, row_count, block_len, HEAD_DIM)
    short_rows = short_cache.reshape(2, row_count, short_len, HEAD_DIM)
    fresh = new_kv.reshape(2, 2, row_count, HEAD_DIM)

    weight_rows = head_weight.T
    pieces = 4
    state, aux, wanted, residual_near, gain_near, out_near, head_near = call(
        functools.partial(attention_kernel, pieces),
        [
            ((packed, 128), F32),
            ((3, pairs, HEAD_DIM), F32),
            ((rows, 128), jnp.int32),
            ((rows, width), BF16),
            ((1, width), F32),
            (out_weight.shape, BF16),
            (weight_rows.shape, BF16),
        ],
        [ANY] * 10,
        "attention",
        [
            pltpu.SMEM((row_count,), jnp.int32),
            pltpu.SMEM((row_count,), jnp.int32),
            pltpu.VMEM(flat_queries.shape, BF16),
            pltpu.VMEM(fresh.shape, BF16),
            pltpu.VMEM(long_rows.shape, BF16),
            pltpu.VMEM(short_rows.shape, BF16),
            pltpu.VMEM((pairs, HEAD_DIM), F32),
            pltpu.VMEM((pairs, HEAD_DIM), F32),
            pltpu.SemaphoreType.DMA((11 + pieces,)),
        ],
        moved=12 * 1024 * 1024,
    )(
        lengths,
        flat_queries,
        long_rows,
        short_rows,
        fresh,
        targets,
        residual.reshape(rows, width),
        final_gain.reshape(1, width),
        out_weight,
        weight_rows,
    )
    other = lax.ppermute(state, "ctx", cores)
    spread = call(pair_kernel, [((chips, packed, 128), F32)], [VMEM] * 2, "merge_cores")(
        state, other
    )
    states = lax.all_to_all(spread, "ctx", 0, 0, tiled=True, axis_index_groups=same_core)
    spread = call(project_kernel, [((tp_size, rows, width), F32)], [VMEM] * 3, "project")(
        states, aux, out_near
    )
    parts = lax.all_to_all(spread, "tp", 0, 0, tiled=True)

    theirs, scaled, squares = call(
        functools.partial(other_kernel, share),
        [((chips, rows, padded), F32), ((rows, width), BF16), ((rows, 128), F32)],
        [VMEM] * 4,
        "head_other",
        moved=4 * 1024 * 1024,
    )(parts, residual_near, gain_near, head_near)
    arrived = lax.ppermute(theirs, "ctx", cores)
    mine = call(
        functools.partial(same_kernel, share),
        [((chips, rows, padded), F32)],
        [VMEM] * 3,
        "head_same",
        moved=4 * 1024 * 1024,
    )(scaled, squares, head_near)
    blocks = call(add_kernel, [((chips, rows, padded), F32)], [VMEM] * 2, "add_cores")(
        mine, arrived
    )
    parts = lax.all_to_all(blocks, "ctx", 0, 0, tiled=True, axis_index_groups=same_core)

    devices = ctx_size * tp_size
    logits, spread = call(
        functools.partial(stats_kernel, share, vocab),
        [((rows, padded), F32), ((devices, 128), F32)],
        [VMEM, VMEM],
        "vocab_stats",
    )(wanted, parts)
    everyone = lax.all_to_all(
        spread.reshape(devices, 1, 128), ("ctx", "tp"), 0, 0, tiled=True
    ).reshape(devices, 128)
    scores, chosen = call(
        functools.partial(scores_kernel, share),
        [((row_count, share), F32), ((1, row_count), F32)],
        [VMEM, VMEM],
        "scores",
        near=jax.ShapeDtypeStruct,
    )(everyone, logits)
    return (scores, chosen.reshape(row_count))


def solution(mesh):
    placed = (
        P(None, None, "tp", None),
        P(None, None, None, "tp", None),
        P(None, None, "ctx", "tp", None),
        P(None, None, None, "tp", None),
        P(),
        P(None, None, "ctx"),
        P("tp", "ctx"),
        P("ctx"),
        P("ctx", "tp"),
        P(),
    )
    return jax.shard_map(
        per_device,
        mesh=mesh,
        in_specs=placed,
        out_specs=(P(None, ("tp", "ctx")), P()),
        check_vma=False,
    )
```

```python
import functools

import jax
import jax.numpy as jnp
from jax import lax
from jax.experimental import pallas as pl
from jax.experimental.pallas import tpu as pltpu
from jax.sharding import PartitionSpec as P

D = 8192
HEAD_DIM = 128
SCORE_SCALE = HEAD_DIM ** (-0.5)

NEG_FILL = -1e30
NORM_EPS = 1e-05
CONTRAST_WEIGHT = 0.5
LOG_FLOOR = -2.302585092994046

F32 = jnp.float32
BESIDE = 30 * 10**9
BF16 = jnp.bfloat16
VMEM = pl.BlockSpec(memory_space=pltpu.VMEM)
ANY = pl.BlockSpec(memory_space=pl.ANY)


def dot_rows(left, right):
    return lax.dot_general(left, right, (((1,), (1,)), ((), ())), preferred_element_type=F32)


def iota(shape, axis):
    return lax.broadcasted_iota(jnp.int32, shape, axis)


def finish(copies):
    @pl.when(lax.axis_index("ctx") >= 0)
    def _():
        for copy in copies:
            copy.wait()


def attention_kernel(
    lengths_far,
    queries_far,
    long_far,
    short_far,
    fresh_far,
    targets_far,
    residual_far,
    gain_far,
    state,
    aux,
    wanted,
    residual,
    gain,
    lengths,
    targets,
    queries,
    fresh,
    long_near,
    short_near,
    wide,
    stat,
    sems,
):
    moves = [
        (lengths_far, lengths),
        (queries_far, queries),
        (long_far.at[0], long_near.at[0]),
        (fresh_far, fresh),
        (short_far.at[0], short_near.at[0]),
        (long_far.at[1], long_near.at[1]),
        (short_far.at[1], short_near.at[1]),
        (targets_far, targets),
        (residual_far, residual),
        (gain_far, gain),
    ]
    copies = [pltpu.make_async_copy(*move, sems.at[n]) for n, move in enumerate(moves)]
    for copy in copies:
        copy.start()
    rows, block_len = long_far.shape[1], long_far.shape[2]
    finish(copies[:5])
    query = [queries[0].astype(F32), queries[1].astype(F32)]
    heads = query[0].shape[0] // rows
    key = [fresh[0, 0].astype(F32), fresh[1, 0].astype(F32)]
    value = [fresh[0, 1].astype(F32), fresh[1, 1].astype(F32)]
    position = lax.axis_index("ctx") * block_len + iota((heads, block_len), 1)
    lane = iota((heads, HEAD_DIM), 1)
    kept, kept_short = [], []
    for b in range(rows):
        part = [q[b * heads : (b + 1) * heads] for q in query]
        mask = position < lengths[b]
        scores = dot_rows(part[0].astype(BF16), long_near[0, b]) * SCORE_SCALE
        scores = jnp.where(mask, scores, NEG_FILL)
        top = jnp.max(scores, axis=1, keepdims=True)
        weights = jnp.where(mask, jnp.exp(scores - top), 0.0)
        total = jnp.sum(weights, axis=1, keepdims=True)
        stat[pl.ds(b, heads, stride=rows), :] = jnp.where(lane == 0, top, total)
        kept.append(weights.astype(BF16))
        own = [
            jnp.sum(part[n] * key[n][b : b + 1], axis=1, keepdims=True) * SCORE_SCALE
            for n in range(2)
        ]
        scores = dot_rows(part[1].astype(BF16), short_near[0, b]) * SCORE_SCALE
        top = jnp.max(scores, axis=1, keepdims=True)
        weights = jnp.exp(scores - top)
        final = jnp.maximum(top, own[1])
        older = jnp.exp(top - final)
        newer = jnp.exp(own[1] - final)
        scale = 1.0 / (jnp.sum(weights, axis=1, keepdims=True) * older + newer)
        kept_short.append((weights.astype(BF16), older * scale, newer * scale))
        where = pl.ds(b, heads, stride=rows)
        aux[1, where, :] = jnp.broadcast_to(own[0], (heads, HEAD_DIM))
        aux[2, where, :] = jnp.broadcast_to(value[0][b : b + 1], (heads, HEAD_DIM))
    finish(copies[5:8])
    for b in range(rows):
        where = pl.ds(b, heads, stride=rows)
        wide[where, :] = jnp.dot(kept[b], long_near[1, b], preferred_element_type=F32)
        weights, older, newer = kept_short[b]
        output = jnp.dot(weights, short_near[1, b], preferred_element_type=F32)
        aux[0, where, :] = output * older + newer * value[1][b : b + 1]
    half = HEAD_DIM // 2
    turned = wide[...].T
    state[0:half, :] = jnp.concatenate([turned[:half], turned[half:]], axis=1)
    turned = stat[...].T[:8]
    state[half : half + 8, :] = jnp.concatenate([turned, turned], axis=1)
    row = iota(wanted.shape, 0)
    aim = jnp.zeros(wanted.shape, jnp.int32)
    for b in range(rows):
        aim = jnp.where(lax.rem(row, rows) == b, targets[b], aim)
    wanted[...] = aim
    finish(copies[8:])


def merge_states(parts):
    half = HEAD_DIM // 2
    tops = [part[half : half + 1, :] for part in parts]
    peak = functools.reduce(jnp.maximum, tops)
    factors = [jnp.exp(top - peak) for top in tops]
    total = sum(part[half + 1 : half + 2, :] * f for part, f in zip(parts, factors))
    values = sum(part[0:half, :] * f for part, f in zip(parts, factors))
    return values, peak, total


def packed_stats(peak, total):
    return jnp.where(iota((8, HEAD_DIM), 0) == 0, peak, total)


def pair_kernel(one, two, spread):
    half = HEAD_DIM // 2
    values, peak, total = merge_states([one, two])
    stats = packed_stats(peak, total)
    for k in range(spread.shape[0]):
        spread[k, 0:half, :] = values
        spread[k, half : half + 8, :] = stats


def project_kernel(states, aux, weight, spread):
    half = HEAD_DIM // 2
    values, peak, total = merge_states([states.at[k] for k in range(states.shape[0])])
    blank = jnp.zeros((half - 8, HEAD_DIM), F32)
    turned = jnp.concatenate([values, packed_stats(peak, total), blank], axis=0).T
    left, right = turned[:half], turned[half:]
    lane = iota((half, HEAD_DIM), 1)
    output = jnp.where(lane < half, left, pltpu.roll(right, half, 1))
    peak, total = left[:, half : half + 1], left[:, half + 1 : half + 2]
    own = aux[1][:, 0:1]
    final = jnp.maximum(peak, own)
    older = jnp.exp(peak - final)
    newer = jnp.exp(own - final)
    attended = [(output * older + newer * aux[2]) / (total * older + newer), aux[0]]
    rows = 8
    heads = half // rows
    rows_wide = jnp.concatenate(
        [
            jnp.concatenate([part[h * rows : (h + 1) * rows] for part in attended], axis=0)
            for h in range(heads)
        ],
        axis=1,
    )
    projected = jnp.dot(rows_wide.astype(BF16), weight[...], preferred_element_type=F32)
    for k in range(spread.shape[0]):
        spread[k] = projected


def head_blocks(other, share, left, fill, weight, blocks):
    vocab, padded = weight.shape[0], blocks.shape[2]
    reach = -(-(share + 15) // 128) * 128
    core = lax.rem(lax.axis_index("ctx"), 2)
    which = 1 - core if other else core
    lane = iota((blocks.shape[1], padded), 1)
    for k in range(blocks.shape[0]):
        offset = (2 * k + which) * share
        base = pl.multiple_of(jnp.minimum(offset // 16 * 16, vocab - reach), 16)
        product = dot_rows(left, weight[pl.ds(base, reach), :])
        moved = pltpu.roll(product, lax.rem(reach - (offset - base), reach), 1)[:, :padded]
        blocks[k] = jnp.where(lane < share, moved, fill)


def other_kernel(share, parts, residual, gain, weight, blocks, scaled, squares):
    projected = sum(parts[k] for k in range(parts.shape[0]))
    stream = residual[...].astype(F32) + projected
    fill = jnp.sum(stream * stream, axis=1, keepdims=True)
    squares[...] = jnp.broadcast_to(fill, squares.shape)
    left = (stream * gain[...]).astype(BF16)
    scaled[...] = left
    head_blocks(True, share, left, fill, weight, blocks)


def same_kernel(share, scaled, squares, weight, blocks):
    head_blocks(False, share, scaled[...], squares[:, 0:1], weight, blocks)


def add_kernel(one, two, out):
    out[...] = one[...] + two[...]


def column_of(values, rows):
    shape = (rows, values.shape[1])
    return jnp.sum(jnp.where(iota(shape, 0) == iota(shape, 1), values, 0.0), axis=1, keepdims=True)


def stats_kernel(share, vocab, wanted, parts, logits, spread):
    rows, padded = logits.shape
    summed = sum(parts[k] for k in range(parts.shape[0]))
    inverse = lax.rsqrt(summed[:, share : share + 1] * (1.0 / D) + NORM_EPS)
    lane = iota((rows, padded), 1)
    valid = lane < share
    local = summed * inverse
    logits[...] = local
    peak = jnp.max(jnp.where(valid, local, -jnp.inf), axis=1, keepdims=True)
    total = jnp.sum(jnp.where(valid, jnp.exp(local - peak), 0.0), axis=1, keepdims=True)
    start = lax.axis_index("tp") * vocab + lax.axis_index("ctx") * share
    hit = jnp.logical_and(valid, lane + start == wanted[:, 0:1])
    picks = jnp.sum(jnp.where(hit, local, 0.0), axis=1, keepdims=True)
    place = iota((rows, 128), 1)
    mixed = jnp.where(place < rows, peak, jnp.where(place < 2 * rows, total, picks))
    keep = jnp.logical_and(lax.rem(place, rows) == iota((rows, 128), 0), place < 3 * rows)
    line = jnp.sum(jnp.where(keep, mixed, 0.0), axis=0, keepdims=True)
    spread[...] = jnp.broadcast_to(line, spread.shape)


def scores_kernel(share, everyone, logits, scores, chosen):
    rows = logits.shape[0]
    half = rows // 2
    data = everyone[...]
    peak = jnp.max(data, axis=0, keepdims=True)
    scale = jnp.exp(data - peak)
    lane = iota(peak.shape, 1)
    total = jnp.sum(pltpu.roll(scale, rows, 1) * data, axis=0, keepdims=True)
    total = jnp.where(lane < rows, pltpu.roll(total, 128 - rows, 1), 1.0)
    picks = pltpu.roll(jnp.sum(data, axis=0, keepdims=True), 128 - 2 * rows, 1)
    lse = peak + jnp.log(total)
    picked = picks - lse
    line = (
        (1.0 + CONTRAST_WEIGHT) * picked
        - CONTRAST_WEIGHT * pltpu.roll(picked, 128 - half, 1)
        + jnp.minimum(0.0, picks - peak - LOG_FLOOR)
    )
    chosen[...] = line[:, :half]
    logp = logits[...] - column_of(lse, rows)
    top = column_of(peak, rows)
    result = (
        (1.0 + CONTRAST_WEIGHT) * logp[:half]
        - CONTRAST_WEIGHT * logp[half:]
        + jnp.minimum(0.0, logits[:half] - top[:half] - LOG_FLOOR)
    )
    scores[...] = result[:, :share]


def call(kernel, out, in_specs, name, scratch=(), flops=0, moved=0, near=pltpu.VMEM):
    outs = [near(shape, kind) for shape, kind in out]
    specs = [VMEM] * len(outs)
    run = pl.pallas_call(
        kernel,
        out_shape=outs if len(outs) > 1 else outs[0],
        in_specs=in_specs,
        out_specs=specs if len(outs) > 1 else specs[0],
        scratch_shapes=list(scratch),
        name=name,
        cost_estimate=pl.CostEstimate(flops=flops, bytes_accessed=moved, transcendentals=0),
        compiler_params=pltpu.CompilerParams(vmem_limit_bytes=16 * 1024 * 1024),
    )

    def pinned(*operands):
        return run(
            *(
                pltpu.with_memory_space_constraint(operand, pltpu.HBM) if spec is ANY else operand
                for operand, spec in zip(operands, in_specs)
            )
        )

    return pinned


def per_device(
    queries,
    new_kv,
    long_cache,
    short_cache,
    lengths,
    residual,
    out_weight,
    final_gain,
    head_weight,
    targets,
):
    row_count, heads = queries.shape[1], queries.shape[2]
    block_len, short_len = long_cache.shape[2], short_cache.shape[2]
    width, vocab = residual.shape[2], head_weight.shape[1]
    ctx_size, tp_size = lax.axis_size("ctx"), lax.axis_size("tp")
    chips = ctx_size // 2
    rows = 2 * row_count
    share = vocab // ctx_size
    padded = -(-(share + 1) // 128) * 128
    pairs = row_count * heads
    packed = HEAD_DIM // 2 + 8
    cores = [(i, i ^ 1) for i in range(ctx_size)]
    same_core = [list(range(which, ctx_size, 2)) for which in range(2)]

    flat_queries = queries.reshape(2, pairs, HEAD_DIM)
    long_rows = long_cache.reshape(2, row_count, block_len, HEAD_DIM)
    short_rows = short_cache.reshape(2, row_count, short_len, HEAD_DIM)
    fresh = new_kv.reshape(2, 2, row_count, HEAD_DIM)

    weight_rows = head_weight.T
    state, aux, wanted, residual_near, gain_near = call(
        attention_kernel,
        [
            ((packed, 128), F32),
            ((3, pairs, HEAD_DIM), F32),
            ((rows, 128), jnp.int32),
            ((rows, width), BF16),
            ((1, width), F32),
        ],
        [ANY] * 8,
        "attention",
        [
            pltpu.SMEM((row_count,), jnp.int32),
            pltpu.SMEM((row_count,), jnp.int32),
            pltpu.VMEM(flat_queries.shape, BF16),
            pltpu.VMEM(fresh.shape, BF16),
            pltpu.VMEM(long_rows.shape, BF16),
            pltpu.VMEM(short_rows.shape, BF16),
            pltpu.VMEM((pairs, HEAD_DIM), F32),
            pltpu.VMEM((pairs, HEAD_DIM), F32),
            pltpu.SemaphoreType.DMA((10,)),
        ],
        moved=3 * 1024 * 1024,
    )(
        lengths,
        flat_queries,
        long_rows,
        short_rows,
        fresh,
        targets,
        residual.reshape(rows, width),
        final_gain.reshape(1, width),
    )
    other = lax.ppermute(state, "ctx", cores)
    spread = call(pair_kernel, [((chips, packed, 128), F32)], [VMEM] * 2, "merge_cores", flops=BESIDE)(
        state, other
    )
    states = lax.all_to_all(spread, "ctx", 0, 0, tiled=True, axis_index_groups=same_core)
    spread = call(project_kernel, [((tp_size, rows, width), F32)], [VMEM] * 3, "project", flops=BESIDE)(
        states, aux, out_weight
    )
    parts = lax.all_to_all(spread, "tp", 0, 0, tiled=True)

    theirs, scaled, squares = call(
        functools.partial(other_kernel, share),
        [((chips, rows, padded), F32), ((rows, width), BF16), ((rows, 128), F32)],
        [VMEM] * 4,
        "head_other",
        moved=4 * 1024 * 1024,
    )(parts, residual_near, gain_near, weight_rows)
    arrived = lax.ppermute(theirs, "ctx", cores)
    mine = call(
        functools.partial(same_kernel, share),
        [((chips, rows, padded), F32)],
        [VMEM] * 3,
        "head_same",
        moved=4 * 1024 * 1024,
    )(scaled, squares, weight_rows)
    blocks = call(add_kernel, [((chips, rows, padded), F32)], [VMEM] * 2, "add_cores")(
        mine, arrived
    )
    parts = lax.all_to_all(blocks, "ctx", 0, 0, tiled=True, axis_index_groups=same_core)

    devices = ctx_size * tp_size
    logits, spread = call(
        functools.partial(stats_kernel, share, vocab),
        [((rows, padded), F32), ((devices, 128), F32)],
        [VMEM, VMEM],
        "vocab_stats",
    )(wanted, parts)
    everyone = lax.all_to_all(
        spread.reshape(devices, 1, 128), ("ctx", "tp"), 0, 0, tiled=True
    ).reshape(devices, 128)
    scores, chosen = call(
        functools.partial(scores_kernel, share),
        [((row_count, share), F32), ((1, row_count), F32)],
        [VMEM, VMEM],
        "scores",
        near=jax.ShapeDtypeStruct,
    )(everyone, logits)
    return (scores, chosen.reshape(row_count))


def solution(mesh):
    placed = (
        P(None, None, "tp", None),
        P(None, None, None, "tp", None),
        P(None, None, "ctx", "tp", None),
        P(None, None, None, "tp", None),
        P(),
        P(None, None, "ctx"),
        P("tp", "ctx"),
        P("ctx"),
        P("ctx", "tp"),
        P(),
    )
    return jax.shard_map(
        per_device,
        mesh=mesh,
        in_specs=placed,
        out_specs=(P(None, ("tp", "ctx")), P()),
        check_vma=False,
    )
```

```python
import functools

import jax
import jax.numpy as jnp
from jax import lax
from jax.experimental import pallas as pl
from jax.experimental.pallas import tpu as pltpu
from jax.sharding import PartitionSpec as P

D = 8192
HEAD_DIM = 128
SCORE_SCALE = HEAD_DIM ** (-0.5)

NEG_FILL = -1e30
NORM_EPS = 1e-05
CONTRAST_WEIGHT = 0.5
LOG_FLOOR = -2.302585092994046

F32 = jnp.float32
BESIDE = 30 * 10**9
BF16 = jnp.bfloat16
VMEM = pl.BlockSpec(memory_space=pltpu.VMEM)
ANY = pl.BlockSpec(memory_space=pl.ANY)


def dot_rows(left, right):
    return lax.dot_general(left, right, (((1,), (1,)), ((), ())), preferred_element_type=F32)


def iota(shape, axis):
    return lax.broadcasted_iota(jnp.int32, shape, axis)


def finish(copies):
    @pl.when(lax.axis_index("ctx") >= 0)
    def _():
        for copy in copies:
            copy.wait()


def attention_kernel(
    lengths_far,
    queries_far,
    long_far,
    short_far,
    fresh_far,
    targets_far,
    residual_far,
    gain_far,
    state,
    aux,
    wanted,
    residual,
    gain,
    lengths,
    targets,
    queries,
    fresh,
    long_near,
    short_near,
    wide,
    stat,
    sems,
):
    moves = [
        (lengths_far, lengths),
        (queries_far, queries),
        (long_far.at[0], long_near.at[0]),
        (fresh_far, fresh),
        (short_far.at[0], short_near.at[0]),
        (long_far.at[1], long_near.at[1]),
        (short_far.at[1], short_near.at[1]),
        (targets_far, targets),
        (residual_far, residual),
        (gain_far, gain),
    ]
    copies = [pltpu.make_async_copy(*move, sems.at[n]) for n, move in enumerate(moves)]
    for copy in copies:
        copy.start()
    rows, block_len = long_far.shape[1], long_far.shape[2]
    finish(copies[:5])
    query = [queries[0].astype(F32), queries[1].astype(F32)]
    heads = query[0].shape[0] // rows
    key = [fresh[0, 0].astype(F32), fresh[1, 0].astype(F32)]
    value = [fresh[0, 1].astype(F32), fresh[1, 1].astype(F32)]
    position = lax.axis_index("ctx") * block_len + iota((heads, block_len), 1)
    lane = iota((heads, HEAD_DIM), 1)
    kept, kept_short = [], []
    for b in range(rows):
        part = [q[b * heads : (b + 1) * heads] for q in query]
        mask = position < lengths[b]
        scores = dot_rows(part[0].astype(BF16), long_near[0, b]) * SCORE_SCALE
        scores = jnp.where(mask, scores, NEG_FILL)
        top = jnp.max(scores, axis=1, keepdims=True)
        weights = jnp.where(mask, jnp.exp(scores - top), 0.0)
        total = jnp.sum(weights, axis=1, keepdims=True)
        stat[pl.ds(b, heads, stride=rows), :] = jnp.where(lane == 0, top, total)
        kept.append(weights.astype(BF16))
        own = [
            jnp.sum(part[n] * key[n][b : b + 1], axis=1, keepdims=True) * SCORE_SCALE
            for n in range(2)
        ]
        scores = dot_rows(part[1].astype(BF16), short_near[0, b]) * SCORE_SCALE
        top = jnp.max(scores, axis=1, keepdims=True)
        weights = jnp.exp(scores - top)
        final = jnp.maximum(top, own[1])
        older = jnp.exp(top - final)
        newer = jnp.exp(own[1] - final)
        scale = 1.0 / (jnp.sum(weights, axis=1, keepdims=True) * older + newer)
        kept_short.append((weights.astype(BF16), older * scale, newer * scale))
        where = pl.ds(b, heads, stride=rows)
        aux[1, where, :] = jnp.broadcast_to(own[0], (heads, HEAD_DIM))
        aux[2, where, :] = jnp.broadcast_to(value[0][b : b + 1], (heads, HEAD_DIM))
    finish(copies[5:8])
    for b in range(rows):
        where = pl.ds(b, heads, stride=rows)
        wide[where, :] = jnp.dot(kept[b], long_near[1, b], preferred_element_type=F32)
        weights, older, newer = kept_short[b]
        output = jnp.dot(weights, short_near[1, b], preferred_element_type=F32)
        aux[0, where, :] = output * older + newer * value[1][b : b + 1]
    half = HEAD_DIM // 2
    turned = wide[...].T
    state[0:half, :] = jnp.concatenate([turned[:half], turned[half:]], axis=1)
    turned = stat[...].T[:8]
    state[half : half + 8, :] = jnp.concatenate([turned, turned], axis=1)
    row = iota(wanted.shape, 0)
    aim = jnp.zeros(wanted.shape, jnp.int32)
    for b in range(rows):
        aim = jnp.where(lax.rem(row, rows) == b, targets[b], aim)
    wanted[...] = aim
    finish(copies[8:])


def merge_states(parts):
    half = HEAD_DIM // 2
    tops = [part[half : half + 1, :] for part in parts]
    peak = functools.reduce(jnp.maximum, tops)
    factors = [jnp.exp(top - peak) for top in tops]
    total = sum(part[half + 1 : half + 2, :] * f for part, f in zip(parts, factors))
    values = sum(part[0:half, :] * f for part, f in zip(parts, factors))
    return values, peak, total


def packed_stats(peak, total):
    return jnp.where(iota((8, HEAD_DIM), 0) == 0, peak, total)


def join_kernel(*refs):
    half = HEAD_DIM // 2
    values, peak, total = merge_states(refs[:-1])
    refs[-1][0:half, :] = values
    refs[-1][half : half + 8, :] = packed_stats(peak, total)


def project_kernel(s0, s1, s2, s3, aux, weight, spread):
    half = HEAD_DIM // 2
    values, peak, total = merge_states([s0, s1, s2, s3])
    blank = jnp.zeros((half - 8, HEAD_DIM), F32)
    turned = jnp.concatenate([values, packed_stats(peak, total), blank], axis=0).T
    left, right = turned[:half], turned[half:]
    lane = iota((half, HEAD_DIM), 1)
    output = jnp.where(lane < half, left, pltpu.roll(right, half, 1))
    peak, total = left[:, half : half + 1], left[:, half + 1 : half + 2]
    own = aux[1][:, 0:1]
    final = jnp.maximum(peak, own)
    older = jnp.exp(peak - final)
    newer = jnp.exp(own - final)
    attended = [(output * older + newer * aux[2]) / (total * older + newer), aux[0]]
    rows = 8
    heads = half // rows
    rows_wide = jnp.concatenate(
        [
            jnp.concatenate([part[h * rows : (h + 1) * rows] for part in attended], axis=0)
            for h in range(heads)
        ],
        axis=1,
    )
    projected = jnp.dot(rows_wide.astype(BF16), weight[...], preferred_element_type=F32)
    for k in range(spread.shape[0]):
        spread[k] = projected


def head_blocks(other, share, left, fill, weight, blocks):
    vocab, padded = weight.shape[0], blocks.shape[2]
    reach = -(-(share + 15) // 128) * 128
    core = lax.rem(lax.axis_index("ctx"), 2)
    which = 1 - core if other else core
    lane = iota((blocks.shape[1], padded), 1)
    for k in range(blocks.shape[0]):
        offset = (2 * k + which) * share
        base = pl.multiple_of(jnp.minimum(offset // 16 * 16, vocab - reach), 16)
        product = dot_rows(left, weight[pl.ds(base, reach), :])
        moved = pltpu.roll(product, lax.rem(reach - (offset - base), reach), 1)[:, :padded]
        blocks[k] = jnp.where(lane < share, moved, fill)


def other_kernel(share, parts, residual, gain, weight, blocks, scaled, squares):
    projected = sum(parts[k] for k in range(parts.shape[0]))
    stream = residual[...].astype(F32) + projected
    fill = jnp.sum(stream * stream, axis=1, keepdims=True)
    squares[...] = jnp.broadcast_to(fill, squares.shape)
    left = (stream * gain[...]).astype(BF16)
    scaled[...] = left
    head_blocks(True, share, left, fill, weight, blocks)


def same_kernel(share, scaled, squares, weight, blocks):
    head_blocks(False, share, scaled[...], squares[:, 0:1], weight, blocks)


def add_kernel(one, two, out):
    out[...] = one[...] + two[...]


def column_of(values, rows):
    shape = (rows, values.shape[1])
    return jnp.sum(jnp.where(iota(shape, 0) == iota(shape, 1), values, 0.0), axis=1, keepdims=True)


def stats_kernel(share, vocab, wanted, parts, logits, spread):
    rows, padded = logits.shape
    summed = sum(parts[k] for k in range(parts.shape[0]))
    inverse = lax.rsqrt(summed[:, share : share + 1] * (1.0 / D) + NORM_EPS)
    lane = iota((rows, padded), 1)
    valid = lane < share
    local = summed * inverse
    logits[...] = local
    peak = jnp.max(jnp.where(valid, local, -jnp.inf), axis=1, keepdims=True)
    total = jnp.sum(jnp.where(valid, jnp.exp(local - peak), 0.0), axis=1, keepdims=True)
    start = lax.axis_index("tp") * vocab + lax.axis_index("ctx") * share
    hit = jnp.logical_and(valid, lane + start == wanted[:, 0:1])
    picks = jnp.sum(jnp.where(hit, local, 0.0), axis=1, keepdims=True)
    place = iota((rows, 128), 1)
    mixed = jnp.where(place < rows, peak, jnp.where(place < 2 * rows, total, picks))
    keep = jnp.logical_and(lax.rem(place, rows) == iota((rows, 128), 0), place < 3 * rows)
    line = jnp.sum(jnp.where(keep, mixed, 0.0), axis=0, keepdims=True)
    spread[...] = jnp.broadcast_to(line, spread.shape)


def join_stats(rows, one, two, spread):
    a, b = one[0:1, :], two[0:1, :]
    peak = jnp.maximum(a, b)
    fa, fb = jnp.exp(a - peak), jnp.exp(b - peak)
    total = a * pltpu.roll(fa, rows, 1) + b * pltpu.roll(fb, rows, 1)
    lane = iota(peak.shape, 1)
    line = jnp.where(lane < rows, peak, jnp.where(lane < 2 * rows, total, a + b))
    spread[...] = jnp.broadcast_to(line, spread.shape)


def scores_kernel(share, everyone, logits, scores, chosen):
    rows = logits.shape[0]
    half = rows // 2
    data = everyone[...]
    peak = jnp.max(data, axis=0, keepdims=True)
    scale = jnp.exp(data - peak)
    lane = iota(peak.shape, 1)
    total = jnp.sum(pltpu.roll(scale, rows, 1) * data, axis=0, keepdims=True)
    total = jnp.where(lane < rows, pltpu.roll(total, 128 - rows, 1), 1.0)
    picks = pltpu.roll(jnp.sum(data, axis=0, keepdims=True), 128 - 2 * rows, 1)
    lse = peak + jnp.log(total)
    picked = picks - lse
    line = (
        (1.0 + CONTRAST_WEIGHT) * picked
        - CONTRAST_WEIGHT * pltpu.roll(picked, 128 - half, 1)
        + jnp.minimum(0.0, picks - peak - LOG_FLOOR)
    )
    chosen[...] = line[:, :half]
    logp = logits[...] - column_of(lse, rows)
    top = column_of(peak, rows)
    result = (
        (1.0 + CONTRAST_WEIGHT) * logp[:half]
        - CONTRAST_WEIGHT * logp[half:]
        + jnp.minimum(0.0, logits[:half] - top[:half] - LOG_FLOOR)
    )
    scores[...] = result[:, :share]


def call(kernel, out, in_specs, name, scratch=(), flops=0, moved=0, near=pltpu.VMEM):
    outs = [near(shape, kind) for shape, kind in out]
    specs = [VMEM] * len(outs)
    run = pl.pallas_call(
        kernel,
        out_shape=outs if len(outs) > 1 else outs[0],
        in_specs=in_specs,
        out_specs=specs if len(outs) > 1 else specs[0],
        scratch_shapes=list(scratch),
        name=name,
        cost_estimate=pl.CostEstimate(flops=flops, bytes_accessed=moved, transcendentals=0),
        compiler_params=pltpu.CompilerParams(vmem_limit_bytes=16 * 1024 * 1024),
    )

    def pinned(*operands):
        return run(
            *(
                pltpu.with_memory_space_constraint(operand, pltpu.HBM) if spec is ANY else operand
                for operand, spec in zip(operands, in_specs)
            )
        )

    return pinned


def per_device(
    queries,
    new_kv,
    long_cache,
    short_cache,
    lengths,
    residual,
    out_weight,
    final_gain,
    head_weight,
    targets,
):
    row_count, heads = queries.shape[1], queries.shape[2]
    block_len, short_len = long_cache.shape[2], short_cache.shape[2]
    width, vocab = residual.shape[2], head_weight.shape[1]
    ctx_size, tp_size = lax.axis_size("ctx"), lax.axis_size("tp")
    chips = ctx_size // 2
    rows = 2 * row_count
    share = vocab // ctx_size
    padded = -(-(share + 1) // 128) * 128
    pairs = row_count * heads
    packed = HEAD_DIM // 2 + 8
    cores = [(i, i ^ 1) for i in range(ctx_size)]
    same_core = [list(range(which, ctx_size, 2)) for which in range(2)]

    flat_queries = queries.reshape(2, pairs, HEAD_DIM)
    long_rows = long_cache.reshape(2, row_count, block_len, HEAD_DIM)
    short_rows = short_cache.reshape(2, row_count, short_len, HEAD_DIM)
    fresh = new_kv.reshape(2, 2, row_count, HEAD_DIM)

    weight_rows = head_weight.T
    state, aux, wanted, residual_near, gain_near = call(
        attention_kernel,
        [
            ((packed, 128), F32),
            ((3, pairs, HEAD_DIM), F32),
            ((rows, 128), jnp.int32),
            ((rows, width), BF16),
            ((1, width), F32),
        ],
        [ANY] * 8,
        "attention",
        [
            pltpu.SMEM((row_count,), jnp.int32),
            pltpu.SMEM((row_count,), jnp.int32),
            pltpu.VMEM(flat_queries.shape, BF16),
            pltpu.VMEM(fresh.shape, BF16),
            pltpu.VMEM(long_rows.shape, BF16),
            pltpu.VMEM(short_rows.shape, BF16),
            pltpu.VMEM((pairs, HEAD_DIM), F32),
            pltpu.VMEM((pairs, HEAD_DIM), F32),
            pltpu.SemaphoreType.DMA((10,)),
        ],
        moved=3 * 1024 * 1024,
    )(
        lengths,
        flat_queries,
        long_rows,
        short_rows,
        fresh,
        targets,
        residual.reshape(rows, width),
        final_gain.reshape(1, width),
    )
    other = lax.ppermute(state, "ctx", cores)
    def ring(value, masks):
        return [
            lax.ppermute(value, "ctx", [(i, i ^ m) for i in range(ctx_size)]) for m in masks
        ]

    state = call(join_kernel, [((packed, 128), F32)], [VMEM] * 2, "merge_cores", flops=BESIDE)(
        state, other
    )
    state = call(join_kernel, [((packed, 128), F32)], [VMEM] * 4, "merge_y", flops=BESIDE)(
        state, *ring(state, (2, 6, 4))
    )
    spread = call(
        project_kernel, [((tp_size, rows, width), F32)], [VMEM] * 6, "project", flops=BESIDE
    )(state, *ring(state, (8, 24, 16)), aux, out_weight)
    parts = lax.all_to_all(spread, "tp", 0, 0, tiled=True)

    theirs, scaled, squares = call(
        functools.partial(other_kernel, share),
        [((chips, rows, padded), F32), ((rows, width), BF16), ((rows, 128), F32)],
        [VMEM] * 4,
        "head_other",
        moved=4 * 1024 * 1024,
    )(parts, residual_near, gain_near, weight_rows)
    arrived = lax.ppermute(theirs, "ctx", cores)
    mine = call(
        functools.partial(same_kernel, share),
        [((chips, rows, padded), F32)],
        [VMEM] * 3,
        "head_same",
        moved=4 * 1024 * 1024,
    )(scaled, squares, weight_rows)
    blocks = call(add_kernel, [((chips, rows, padded), F32)], [VMEM] * 2, "add_cores")(
        mine, arrived
    )
    parts = lax.all_to_all(blocks, "ctx", 0, 0, tiled=True, axis_index_groups=same_core)

    devices = chips * tp_size
    logits, line = call(
        functools.partial(stats_kernel, share, vocab),
        [((rows, padded), F32), ((8, 128), F32)],
        [VMEM, VMEM],
        "vocab_stats",
    )(wanted, parts)
    arrived = lax.ppermute(line, "ctx", cores)
    spread = call(
        functools.partial(join_stats, rows), [((devices, 128), F32)], [VMEM] * 2, "join_stats"
    )(line, arrived)
    groups = [
        [c * tp_size + t for c in range(which, ctx_size, 2) for t in range(tp_size)]
        for which in range(2)
    ]
    everyone = lax.all_to_all(
        spread.reshape(devices, 1, 128), ("ctx", "tp"), 0, 0, tiled=True, axis_index_groups=groups
    ).reshape(devices, 128)
    scores, chosen = call(
        functools.partial(scores_kernel, share),
        [((row_count, share), F32), ((1, row_count), F32)],
        [VMEM, VMEM],
        "scores",
        near=jax.ShapeDtypeStruct,
    )(everyone, logits)
    return (scores, chosen.reshape(row_count))


def solution(mesh):
    placed = (
        P(None, None, "tp", None),
        P(None, None, None, "tp", None),
        P(None, None, "ctx", "tp", None),
        P(None, None, None, "tp", None),
        P(),
        P(None, None, "ctx"),
        P("tp", "ctx"),
        P("ctx"),
        P("ctx", "tp"),
        P(),
    )
    return jax.shard_map(
        per_device,
        mesh=mesh,
        in_specs=placed,
        out_specs=(P(None, ("tp", "ctx")), P()),
        check_vma=False,
    )
```

```python
import functools

import jax
import jax.numpy as jnp
from jax import lax
from jax.experimental import pallas as pl
from jax.experimental.pallas import tpu as pltpu
from jax.sharding import PartitionSpec as P

D = 8192
HEAD_DIM = 128
SCORE_SCALE = HEAD_DIM ** (-0.5)

NEG_FILL = -1e30
NORM_EPS = 1e-05
CONTRAST_WEIGHT = 0.5
LOG_FLOOR = -2.302585092994046

F32 = jnp.float32
BESIDE = 30 * 10**9
BF16 = jnp.bfloat16
VMEM = pl.BlockSpec(memory_space=pltpu.VMEM)
ANY = pl.BlockSpec(memory_space=pl.ANY)


def dot_rows(left, right):
    return lax.dot_general(left, right, (((1,), (1,)), ((), ())), preferred_element_type=F32)


def iota(shape, axis):
    return lax.broadcasted_iota(jnp.int32, shape, axis)


def finish(copies):
    @pl.when(lax.axis_index("ctx") >= 0)
    def _():
        for copy in copies:
            copy.wait()


def begin(moves, sems):
    copies = [pltpu.make_async_copy(*move, sems.at[n]) for n, move in enumerate(moves)]
    for copy in copies:
        copy.start()
    return copies


def long_kernel(
    lengths_far, queries_far, cache_far, state, lengths, queries, cache, wide, stat, sems
):
    copies = begin(
        [
            (lengths_far, lengths),
            (queries_far.at[0], queries),
            (cache_far.at[0], cache.at[0]),
            (cache_far.at[1], cache.at[1]),
        ],
        sems,
    )
    rows, block_len = cache.shape[1], cache.shape[2]
    finish(copies[:3])
    query = queries[...].astype(F32)
    heads = query.shape[0] // rows
    position = lax.axis_index("ctx") * block_len + iota((heads, block_len), 1)
    lane = iota((heads, HEAD_DIM), 1)
    kept = []
    for b in range(rows):
        mask = position < lengths[b]
        scores = dot_rows(query[b * heads : (b + 1) * heads].astype(BF16), cache[0, b])
        scores = jnp.where(mask, scores * SCORE_SCALE, NEG_FILL)
        top = jnp.max(scores, axis=1, keepdims=True)
        weights = jnp.where(mask, jnp.exp(scores - top), 0.0)
        total = jnp.sum(weights, axis=1, keepdims=True)
        stat[pl.ds(b, heads, stride=rows), :] = jnp.where(lane == 0, top, total)
        kept.append(weights.astype(BF16))
    finish(copies[3:])
    for b in range(rows):
        wide[pl.ds(b, heads, stride=rows), :] = jnp.dot(
            kept[b], cache[1, b], preferred_element_type=F32
        )
    half = HEAD_DIM // 2
    turned = wide[...].T
    state[0:half, :] = jnp.concatenate([turned[:half], turned[half:]], axis=1)
    turned = stat[...].T[:8]
    state[half : half + 8, :] = jnp.concatenate([turned, turned], axis=1)


def short_kernel(
    queries_far,
    cache_far,
    fresh_far,
    targets_far,
    residual_far,
    gain_far,
    aux,
    wanted,
    residual,
    gain,
    targets,
    queries,
    fresh,
    cache,
    sems,
):
    copies = begin(
        [
            (queries_far, queries),
            (fresh_far, fresh),
            (cache_far.at[0], cache.at[0]),
            (cache_far.at[1], cache.at[1]),
            (targets_far, targets),
            (residual_far, residual),
            (gain_far, gain),
        ],
        sems,
    )
    finish(copies)
    rows = cache.shape[1]
    query = [queries[0].astype(F32), queries[1].astype(F32)]
    heads = query[0].shape[0] // rows
    key = [fresh[0, 0].astype(F32), fresh[1, 0].astype(F32)]
    value = [fresh[0, 1].astype(F32), fresh[1, 1].astype(F32)]
    for b in range(rows):
        part = [q[b * heads : (b + 1) * heads] for q in query]
        own = [
            jnp.sum(part[n] * key[n][b : b + 1], axis=1, keepdims=True) * SCORE_SCALE
            for n in range(2)
        ]
        scores = dot_rows(part[1].astype(BF16), cache[0, b]) * SCORE_SCALE
        top = jnp.max(scores, axis=1, keepdims=True)
        weights = jnp.exp(scores - top)
        total = jnp.sum(weights, axis=1, keepdims=True)
        output = jnp.dot(weights.astype(BF16), cache[1, b], preferred_element_type=F32)
        final = jnp.maximum(top, own[1])
        older = jnp.exp(top - final)
        newer = jnp.exp(own[1] - final)
        mixed = output * older + newer * value[1][b : b + 1]
        where = pl.ds(b, heads, stride=rows)
        aux[0, where, :] = mixed / (total * older + newer)
        aux[1, where, :] = jnp.broadcast_to(own[0], (heads, HEAD_DIM))
        aux[2, where, :] = jnp.broadcast_to(value[0][b : b + 1], (heads, HEAD_DIM))
    row = iota(wanted.shape, 0)
    aim = jnp.zeros(wanted.shape, jnp.int32)
    for b in range(rows):
        aim = jnp.where(lax.rem(row, rows) == b, targets[b], aim)
    wanted[...] = aim


def merge_states(parts):
    half = HEAD_DIM // 2
    tops = [part[half : half + 1, :] for part in parts]
    peak = functools.reduce(jnp.maximum, tops)
    factors = [jnp.exp(top - peak) for top in tops]
    total = sum(part[half + 1 : half + 2, :] * f for part, f in zip(parts, factors))
    values = sum(part[0:half, :] * f for part, f in zip(parts, factors))
    return values, peak, total


def packed_stats(peak, total):
    return jnp.where(iota((8, HEAD_DIM), 0) == 0, peak, total)


def join_kernel(*refs):
    half = HEAD_DIM // 2
    values, peak, total = merge_states(refs[:-1])
    refs[-1][0:half, :] = values
    refs[-1][half : half + 8, :] = packed_stats(peak, total)


def project_kernel(s0, s1, s2, s3, aux, weight, spread):
    half = HEAD_DIM // 2
    values, peak, total = merge_states([s0, s1, s2, s3])
    blank = jnp.zeros((half - 8, HEAD_DIM), F32)
    turned = jnp.concatenate([values, packed_stats(peak, total), blank], axis=0).T
    left, right = turned[:half], turned[half:]
    lane = iota((half, HEAD_DIM), 1)
    output = jnp.where(lane < half, left, pltpu.roll(right, half, 1))
    peak, total = left[:, half : half + 1], left[:, half + 1 : half + 2]
    own = aux[1][:, 0:1]
    final = jnp.maximum(peak, own)
    older = jnp.exp(peak - final)
    newer = jnp.exp(own - final)
    attended = [(output * older + newer * aux[2]) / (total * older + newer), aux[0]]
    rows = 8
    heads = half // rows
    rows_wide = jnp.concatenate(
        [
            jnp.concatenate([part[h * rows : (h + 1) * rows] for part in attended], axis=0)
            for h in range(heads)
        ],
        axis=1,
    )
    projected = jnp.dot(rows_wide.astype(BF16), weight[...], preferred_element_type=F32)
    for k in range(spread.shape[0]):
        spread[k] = projected


def head_blocks(other, share, left, fill, weight, blocks):
    vocab, padded = weight.shape[0], blocks.shape[2]
    fetched = -(-(share + 15) // 16) * 16
    reach = -(-fetched // 128) * 128
    blank = jnp.zeros((blocks.shape[1], reach - fetched), F32)
    core = lax.rem(lax.axis_index("ctx"), 2)
    which = 1 - core if other else core
    lane = iota((blocks.shape[1], padded), 1)
    for k in range(blocks.shape[0]):
        offset = (2 * k + which) * share
        base = pl.multiple_of(jnp.minimum(offset // 16 * 16, vocab - fetched), 16)
        product = jnp.concatenate(
            [
                dot_rows(left, weight[pl.ds(base, padded), :]),
                dot_rows(left, weight[pl.ds(base + padded, fetched - padded), :]),
                blank,
            ],
            axis=1,
        )
        moved = pltpu.roll(product, lax.rem(reach - (offset - base), reach), 1)[:, :padded]
        blocks[k] = jnp.where(lane < share, moved, fill)


def other_kernel(share, parts, residual, gain, weight, blocks, scaled, squares):
    projected = sum(parts[k] for k in range(parts.shape[0]))
    stream = residual[...].astype(F32) + projected
    fill = jnp.sum(stream * stream, axis=1, keepdims=True)
    squares[...] = jnp.broadcast_to(fill, squares.shape)
    left = (stream * gain[...]).astype(BF16)
    scaled[...] = left
    head_blocks(True, share, left, fill, weight, blocks)


def same_kernel(share, scaled, squares, weight, blocks):
    head_blocks(False, share, scaled[...], squares[:, 0:1], weight, blocks)


def add_kernel(one, two, out):
    out[...] = one[...] + two[...]


def column_of(values, rows):
    shape = (rows, values.shape[1])
    return jnp.sum(jnp.where(iota(shape, 0) == iota(shape, 1), values, 0.0), axis=1, keepdims=True)


def stats_kernel(share, vocab, wanted, parts, logits, spread):
    rows, padded = logits.shape
    summed = sum(parts[k] for k in range(parts.shape[0]))
    inverse = lax.rsqrt(summed[:, share : share + 1] * (1.0 / D) + NORM_EPS)
    lane = iota((rows, padded), 1)
    valid = lane < share
    local = summed * inverse
    logits[...] = local
    peak = jnp.max(jnp.where(valid, local, -jnp.inf), axis=1, keepdims=True)
    total = jnp.sum(jnp.where(valid, jnp.exp(local - peak), 0.0), axis=1, keepdims=True)
    start = lax.axis_index("tp") * vocab + lax.axis_index("ctx") * share
    hit = jnp.logical_and(valid, lane + start == wanted[:, 0:1])
    picks = jnp.sum(jnp.where(hit, local, 0.0), axis=1, keepdims=True)
    place = iota((rows, 128), 1)
    mixed = jnp.where(place < rows, peak, jnp.where(place < 2 * rows, total, picks))
    keep = jnp.logical_and(lax.rem(place, rows) == iota((rows, 128), 0), place < 3 * rows)
    line = jnp.sum(jnp.where(keep, mixed, 0.0), axis=0, keepdims=True)
    spread[...] = jnp.broadcast_to(line, spread.shape)


def join_stats(rows, one, two, spread):
    a, b = one[0:1, :], two[0:1, :]
    peak = jnp.maximum(a, b)
    fa, fb = jnp.exp(a - peak), jnp.exp(b - peak)
    total = a * pltpu.roll(fa, rows, 1) + b * pltpu.roll(fb, rows, 1)
    lane = iota(peak.shape, 1)
    line = jnp.where(lane < rows, peak, jnp.where(lane < 2 * rows, total, a + b))
    spread[...] = jnp.broadcast_to(line, spread.shape)


def scores_kernel(share, everyone, logits, scores, chosen):
    rows = logits.shape[0]
    half = rows // 2
    data = everyone[...]
    peak = jnp.max(data, axis=0, keepdims=True)
    scale = jnp.exp(data - peak)
    lane = iota(peak.shape, 1)
    total = jnp.sum(pltpu.roll(scale, rows, 1) * data, axis=0, keepdims=True)
    total = jnp.where(lane < rows, pltpu.roll(total, 128 - rows, 1), 1.0)
    picks = pltpu.roll(jnp.sum(data, axis=0, keepdims=True), 128 - 2 * rows, 1)
    lse = peak + jnp.log(total)
    picked = picks - lse
    line = (
        (1.0 + CONTRAST_WEIGHT) * picked
        - CONTRAST_WEIGHT * pltpu.roll(picked, 128 - half, 1)
        + jnp.minimum(0.0, picks - peak - LOG_FLOOR)
    )
    chosen[...] = line[:, :half]
    logp = logits[...] - column_of(lse, rows)
    top = column_of(peak, rows)
    result = (
        (1.0 + CONTRAST_WEIGHT) * logp[:half]
        - CONTRAST_WEIGHT * logp[half:]
        + jnp.minimum(0.0, logits[:half] - top[:half] - LOG_FLOOR)
    )
    scores[...] = result[:, :share]


def call(kernel, out, in_specs, name, scratch=(), flops=0, moved=0, near=pltpu.VMEM):
    outs = [near(shape, kind) for shape, kind in out]
    specs = [VMEM] * len(outs)
    run = pl.pallas_call(
        kernel,
        out_shape=outs if len(outs) > 1 else outs[0],
        in_specs=in_specs,
        out_specs=specs if len(outs) > 1 else specs[0],
        scratch_shapes=list(scratch),
        name=name,
        cost_estimate=pl.CostEstimate(flops=flops, bytes_accessed=moved, transcendentals=0),
        compiler_params=pltpu.CompilerParams(vmem_limit_bytes=16 * 1024 * 1024),
    )

    def pinned(*operands):
        return run(
            *(
                pltpu.with_memory_space_constraint(operand, pltpu.HBM) if spec is ANY else operand
                for operand, spec in zip(operands, in_specs)
            )
        )

    return pinned


def per_device(
    queries,
    new_kv,
    long_cache,
    short_cache,
    lengths,
    residual,
    out_weight,
    final_gain,
    head_weight,
    targets,
):
    row_count, heads = queries.shape[1], queries.shape[2]
    block_len, short_len = long_cache.shape[2], short_cache.shape[2]
    width, vocab = residual.shape[2], head_weight.shape[1]
    ctx_size, tp_size = lax.axis_size("ctx"), lax.axis_size("tp")
    chips = ctx_size // 2
    rows = 2 * row_count
    share = vocab // ctx_size
    padded = -(-(share + 1) // 128) * 128
    pairs = row_count * heads
    packed = HEAD_DIM // 2 + 8
    cores = [(i, i ^ 1) for i in range(ctx_size)]
    same_core = [list(range(which, ctx_size, 2)) for which in range(2)]

    flat_queries = queries.reshape(2, pairs, HEAD_DIM)
    long_rows = long_cache.reshape(2, row_count, block_len, HEAD_DIM)
    short_rows = short_cache.reshape(2, row_count, short_len, HEAD_DIM)
    fresh = new_kv.reshape(2, 2, row_count, HEAD_DIM)

    weight_rows = head_weight.T
    state = call(
        long_kernel,
        [((packed, 128), F32)],
        [ANY] * 3,
        "long_attention",
        [
            pltpu.SMEM((row_count,), jnp.int32),
            pltpu.VMEM((pairs, HEAD_DIM), BF16),
            pltpu.VMEM(long_rows.shape, BF16),
            pltpu.VMEM((pairs, HEAD_DIM), F32),
            pltpu.VMEM((pairs, HEAD_DIM), F32),
            pltpu.SemaphoreType.DMA((4,)),
        ],
        moved=2 * 1024 * 1024,
    )(lengths, flat_queries, long_rows)
    other = lax.ppermute(state, "ctx", cores)
    def ring(value, masks):
        return [
            lax.ppermute(value, "ctx", [(i, i ^ m) for i in range(ctx_size)]) for m in masks
        ]

    state = call(join_kernel, [((packed, 128), F32)], [VMEM] * 2, "merge_cores", flops=BESIDE)(
        state, other
    )
    near_y = ring(state, (2, 6, 4))
    state = call(join_kernel, [((packed, 128), F32)], [VMEM] * 4, "merge_y", flops=BESIDE)(
        state, *near_y
    )
    state, fresh = lax.optimization_barrier((state, fresh))
    near_x = ring(state, (8, 24, 16))
    aux, wanted, residual_near, gain_near = call(
        short_kernel,
        [
            ((3, pairs, HEAD_DIM), F32),
            ((rows, 128), jnp.int32),
            ((rows, width), BF16),
            ((1, width), F32),
        ],
        [ANY] * 6,
        "short_attention",
        [
            pltpu.SMEM((row_count,), jnp.int32),
            pltpu.VMEM(flat_queries.shape, BF16),
            pltpu.VMEM(fresh.shape, BF16),
            pltpu.VMEM(short_rows.shape, BF16),
            pltpu.SemaphoreType.DMA((7,)),
        ],
        moved=1024 * 1024,
    )(
        flat_queries,
        short_rows,
        fresh,
        targets,
        residual.reshape(rows, width),
        final_gain.reshape(1, width),
    )
    spread = call(
        project_kernel, [((tp_size, rows, width), F32)], [VMEM] * 6, "project", flops=BESIDE
    )(state, *near_x, aux, out_weight)
    parts = lax.all_to_all(spread, "tp", 0, 0, tiled=True)

    theirs, scaled, squares = call(
        functools.partial(other_kernel, share),
        [((chips, rows, padded), F32), ((rows, width), BF16), ((rows, 128), F32)],
        [VMEM] * 4,
        "head_other",
        moved=4 * 1024 * 1024,
    )(parts, residual_near, gain_near, weight_rows)
    arrived = lax.ppermute(theirs, "ctx", cores)
    mine = call(
        functools.partial(same_kernel, share),
        [((chips, rows, padded), F32)],
        [VMEM] * 3,
        "head_same",
        moved=4 * 1024 * 1024,
    )(scaled, squares, weight_rows)
    blocks = call(add_kernel, [((chips, rows, padded), F32)], [VMEM] * 2, "add_cores")(
        mine, arrived
    )
    parts = lax.all_to_all(blocks, "ctx", 0, 0, tiled=True, axis_index_groups=same_core)

    devices = chips * tp_size
    logits, line = call(
        functools.partial(stats_kernel, share, vocab),
        [((rows, padded), F32), ((8, 128), F32)],
        [VMEM, VMEM],
        "vocab_stats",
    )(wanted, parts)
    arrived = lax.ppermute(line, "ctx", cores)
    spread = call(
        functools.partial(join_stats, rows), [((devices, 128), F32)], [VMEM] * 2, "join_stats"
    )(line, arrived)
    groups = [
        [c * tp_size + t for c in range(which, ctx_size, 2) for t in range(tp_size)]
        for which in range(2)
    ]
    everyone = lax.all_to_all(
        spread.reshape(devices, 1, 128), ("ctx", "tp"), 0, 0, tiled=True, axis_index_groups=groups
    ).reshape(devices, 128)
    scores, chosen = call(
        functools.partial(scores_kernel, share),
        [((row_count, share), F32), ((1, row_count), F32)],
        [VMEM, VMEM],
        "scores",
        near=jax.ShapeDtypeStruct,
    )(everyone, logits)
    return (scores, chosen.reshape(row_count))


def solution(mesh):
    placed = (
        P(None, None, "tp", None),
        P(None, None, None, "tp", None),
        P(None, None, "ctx", "tp", None),
        P(None, None, None, "tp", None),
        P(),
        P(None, None, "ctx"),
        P("tp", "ctx"),
        P("ctx"),
        P("ctx", "tp"),
        P(),
    )
    return jax.shard_map(
        per_device,
        mesh=mesh,
        in_specs=placed,
        out_specs=(P(None, ("tp", "ctx")), P()),
        check_vma=False,
    )
```

```python
import functools

import jax
import jax.numpy as jnp
from jax import lax
from jax.experimental import pallas as pl
from jax.experimental.pallas import tpu as pltpu
from jax.sharding import PartitionSpec as P

D = 8192
HEAD_DIM = 128
SCORE_SCALE = HEAD_DIM ** (-0.5)

NEG_FILL = -1e30
NORM_EPS = 1e-05
CONTRAST_WEIGHT = 0.5
LOG_FLOOR = -2.302585092994046

F32 = jnp.float32
BESIDE = 30 * 10**9
BF16 = jnp.bfloat16
VMEM = pl.BlockSpec(memory_space=pltpu.VMEM)
ANY = pl.BlockSpec(memory_space=pl.ANY)


def dot_rows(left, right):
    return lax.dot_general(left, right, (((1,), (1,)), ((), ())), preferred_element_type=F32)


def iota(shape, axis):
    return lax.broadcasted_iota(jnp.int32, shape, axis)


def finish(copies):
    @pl.when(lax.axis_index("ctx") >= 0)
    def _():
        for copy in copies:
            copy.wait()


def begin(moves, sems):
    copies = [pltpu.make_async_copy(*move, sems.at[n]) for n, move in enumerate(moves)]
    for copy in copies:
        copy.start()
    return copies


def long_kernel(
    lengths_far, queries_far, cache_far, state, lengths, queries, cache, wide, stat, sems
):
    copies = begin(
        [
            (lengths_far, lengths),
            (queries_far.at[0], queries),
            (cache_far.at[0], cache.at[0]),
            (cache_far.at[1], cache.at[1]),
        ],
        sems,
    )
    rows, block_len = cache.shape[1], cache.shape[2]
    finish(copies[:3])
    query = queries[...].astype(F32)
    heads = query.shape[0] // rows
    position = lax.axis_index("ctx") * block_len + iota((heads, block_len), 1)
    lane = iota((heads, HEAD_DIM), 1)
    kept = []
    for b in range(rows):
        mask = position < lengths[b]
        scores = dot_rows(query[b * heads : (b + 1) * heads].astype(BF16), cache[0, b])
        scores = jnp.where(mask, scores * SCORE_SCALE, NEG_FILL)
        top = jnp.max(scores, axis=1, keepdims=True)
        weights = jnp.where(mask, jnp.exp(scores - top), 0.0)
        total = jnp.sum(weights, axis=1, keepdims=True)
        stat[pl.ds(b, heads, stride=rows), :] = jnp.where(lane == 0, top, total)
        kept.append(weights.astype(BF16))
    finish(copies[3:])
    for b in range(rows):
        wide[pl.ds(b, heads, stride=rows), :] = jnp.dot(
            kept[b], cache[1, b], preferred_element_type=F32
        )
    half = HEAD_DIM // 2
    turned = wide[...].T
    state[0:half, :] = jnp.concatenate([turned[:half], turned[half:]], axis=1)
    turned = stat[...].T[:8]
    state[half : half + 8, :] = jnp.concatenate([turned, turned], axis=1)


def short_kernel(
    queries,
    cache,
    fresh,
    targets_far,
    residual_far,
    gain_far,
    aux,
    wanted,
    residual,
    gain,
    targets,
    sems,
):
    copies = begin(
        [
            (targets_far, targets),
            (residual_far, residual),
            (gain_far, gain),
        ],
        sems,
    )
    rows = cache.shape[1]
    query = [queries[0].astype(F32), queries[1].astype(F32)]
    heads = query[0].shape[0] // rows
    key = [fresh[0, 0].astype(F32), fresh[1, 0].astype(F32)]
    value = [fresh[0, 1].astype(F32), fresh[1, 1].astype(F32)]
    for b in range(rows):
        part = [q[b * heads : (b + 1) * heads] for q in query]
        own = [
            jnp.sum(part[n] * key[n][b : b + 1], axis=1, keepdims=True) * SCORE_SCALE
            for n in range(2)
        ]
        scores = dot_rows(part[1].astype(BF16), cache[0, b]) * SCORE_SCALE
        top = jnp.max(scores, axis=1, keepdims=True)
        weights = jnp.exp(scores - top)
        total = jnp.sum(weights, axis=1, keepdims=True)
        output = jnp.dot(weights.astype(BF16), cache[1, b], preferred_element_type=F32)
        final = jnp.maximum(top, own[1])
        older = jnp.exp(top - final)
        newer = jnp.exp(own[1] - final)
        mixed = output * older + newer * value[1][b : b + 1]
        where = pl.ds(b, heads, stride=rows)
        aux[0, where, :] = mixed / (total * older + newer)
        aux[1, where, :] = jnp.broadcast_to(own[0], (heads, HEAD_DIM))
        aux[2, where, :] = jnp.broadcast_to(value[0][b : b + 1], (heads, HEAD_DIM))
    finish(copies)
    row = iota(wanted.shape, 0)
    aim = jnp.zeros(wanted.shape, jnp.int32)
    for b in range(rows):
        aim = jnp.where(lax.rem(row, rows) == b, targets[b], aim)
    wanted[...] = aim


def merge_states(parts):
    half = HEAD_DIM // 2
    tops = [part[half : half + 1, :] for part in parts]
    peak = functools.reduce(jnp.maximum, tops)
    factors = [jnp.exp(top - peak) for top in tops]
    total = sum(part[half + 1 : half + 2, :] * f for part, f in zip(parts, factors))
    values = sum(part[0:half, :] * f for part, f in zip(parts, factors))
    return values, peak, total


def packed_stats(peak, total):
    return jnp.where(iota((8, HEAD_DIM), 0) == 0, peak, total)


def join_kernel(*refs):
    half = HEAD_DIM // 2
    values, peak, total = merge_states(refs[:-1])
    refs[-1][0:half, :] = values
    refs[-1][half : half + 8, :] = packed_stats(peak, total)


def project_kernel(s0, s1, s2, s3, aux, weight, spread):
    half = HEAD_DIM // 2
    values, peak, total = merge_states([s0, s1, s2, s3])
    blank = jnp.zeros((half - 8, HEAD_DIM), F32)
    turned = jnp.concatenate([values, packed_stats(peak, total), blank], axis=0).T
    left, right = turned[:half], turned[half:]
    lane = iota((half, HEAD_DIM), 1)
    output = jnp.where(lane < half, left, pltpu.roll(right, half, 1))
    peak, total = left[:, half : half + 1], left[:, half + 1 : half + 2]
    own = aux[1][:, 0:1]
    final = jnp.maximum(peak, own)
    older = jnp.exp(peak - final)
    newer = jnp.exp(own - final)
    attended = [(output * older + newer * aux[2]) / (total * older + newer), aux[0]]
    rows = 8
    heads = half // rows
    rows_wide = jnp.concatenate(
        [
            jnp.concatenate([part[h * rows : (h + 1) * rows] for part in attended], axis=0)
            for h in range(heads)
        ],
        axis=1,
    )
    projected = jnp.dot(rows_wide.astype(BF16), weight[...], preferred_element_type=F32)
    for k in range(spread.shape[0]):
        spread[k] = projected


def head_blocks(other, share, left, fill, weight, blocks):
    vocab, padded = weight.shape[0], blocks.shape[2]
    fetched = -(-(share + 15) // 16) * 16
    reach = -(-fetched // 128) * 128
    blank = jnp.zeros((blocks.shape[1], reach - fetched), F32)
    core = lax.rem(lax.axis_index("ctx"), 2)
    which = 1 - core if other else core
    lane = iota((blocks.shape[1], padded), 1)
    for k in range(blocks.shape[0]):
        offset = (2 * k + which) * share
        base = pl.multiple_of(jnp.minimum(offset // 16 * 16, vocab - fetched), 16)
        product = jnp.concatenate(
            [
                dot_rows(left, weight[pl.ds(base, padded), :]),
                dot_rows(left, weight[pl.ds(base + padded, fetched - padded), :]),
                blank,
            ],
            axis=1,
        )
        moved = pltpu.roll(product, lax.rem(reach - (offset - base), reach), 1)[:, :padded]
        blocks[k] = jnp.where(lane < share, moved, fill)


def other_kernel(share, parts, residual, gain, weight, blocks, scaled, squares):
    projected = sum(parts[k] for k in range(parts.shape[0]))
    stream = residual[...].astype(F32) + projected
    fill = jnp.sum(stream * stream, axis=1, keepdims=True)
    squares[...] = jnp.broadcast_to(fill, squares.shape)
    left = (stream * gain[...]).astype(BF16)
    scaled[...] = left
    head_blocks(True, share, left, fill, weight, blocks)


def same_kernel(share, scaled, squares, weight, blocks):
    head_blocks(False, share, scaled[...], squares[:, 0:1], weight, blocks)


def add_kernel(one, two, out):
    out[...] = one[...] + two[...]


def column_of(values, rows):
    shape = (rows, values.shape[1])
    return jnp.sum(jnp.where(iota(shape, 0) == iota(shape, 1), values, 0.0), axis=1, keepdims=True)


def stats_kernel(share, vocab, wanted, parts, logits, spread):
    rows, padded = logits.shape
    summed = sum(parts[k] for k in range(parts.shape[0]))
    inverse = lax.rsqrt(summed[:, share : share + 1] * (1.0 / D) + NORM_EPS)
    lane = iota((rows, padded), 1)
    valid = lane < share
    local = summed * inverse
    logits[...] = local
    peak = jnp.max(jnp.where(valid, local, -jnp.inf), axis=1, keepdims=True)
    total = jnp.sum(jnp.where(valid, jnp.exp(local - peak), 0.0), axis=1, keepdims=True)
    start = lax.axis_index("tp") * vocab + lax.axis_index("ctx") * share
    hit = jnp.logical_and(valid, lane + start == wanted[:, 0:1])
    picks = jnp.sum(jnp.where(hit, local, 0.0), axis=1, keepdims=True)
    place = iota((rows, 128), 1)
    mixed = jnp.where(place < rows, peak, jnp.where(place < 2 * rows, total, picks))
    keep = jnp.logical_and(lax.rem(place, rows) == iota((rows, 128), 0), place < 3 * rows)
    line = jnp.sum(jnp.where(keep, mixed, 0.0), axis=0, keepdims=True)
    spread[...] = jnp.broadcast_to(line, spread.shape)


def join_stats(rows, one, two, spread):
    a, b = one[0:1, :], two[0:1, :]
    peak = jnp.maximum(a, b)
    fa, fb = jnp.exp(a - peak), jnp.exp(b - peak)
    total = a * pltpu.roll(fa, rows, 1) + b * pltpu.roll(fb, rows, 1)
    lane = iota(peak.shape, 1)
    line = jnp.where(lane < rows, peak, jnp.where(lane < 2 * rows, total, a + b))
    spread[...] = jnp.broadcast_to(line, spread.shape)


def scores_kernel(share, everyone, logits, scores, chosen):
    rows = logits.shape[0]
    half = rows // 2
    data = everyone[...]
    peak = jnp.max(data, axis=0, keepdims=True)
    scale = jnp.exp(data - peak)
    lane = iota(peak.shape, 1)
    total = jnp.sum(pltpu.roll(scale, rows, 1) * data, axis=0, keepdims=True)
    total = jnp.where(lane < rows, pltpu.roll(total, 128 - rows, 1), 1.0)
    picks = pltpu.roll(jnp.sum(data, axis=0, keepdims=True), 128 - 2 * rows, 1)
    lse = peak + jnp.log(total)
    picked = picks - lse
    line = (
        (1.0 + CONTRAST_WEIGHT) * picked
        - CONTRAST_WEIGHT * pltpu.roll(picked, 128 - half, 1)
        + jnp.minimum(0.0, picks - peak - LOG_FLOOR)
    )
    chosen[...] = line[:, :half]
    logp = logits[...] - column_of(lse, rows)
    top = column_of(peak, rows)
    result = (
        (1.0 + CONTRAST_WEIGHT) * logp[:half]
        - CONTRAST_WEIGHT * logp[half:]
        + jnp.minimum(0.0, logits[:half] - top[:half] - LOG_FLOOR)
    )
    scores[...] = result[:, :share]


def call(kernel, out, in_specs, name, scratch=(), flops=0, moved=0, near=pltpu.VMEM):
    outs = [near(shape, kind) for shape, kind in out]
    specs = [VMEM] * len(outs)
    run = pl.pallas_call(
        kernel,
        out_shape=outs if len(outs) > 1 else outs[0],
        in_specs=in_specs,
        out_specs=specs if len(outs) > 1 else specs[0],
        scratch_shapes=list(scratch),
        name=name,
        cost_estimate=pl.CostEstimate(flops=flops, bytes_accessed=moved, transcendentals=0),
        compiler_params=pltpu.CompilerParams(vmem_limit_bytes=16 * 1024 * 1024),
    )

    def pinned(*operands):
        return run(
            *(
                pltpu.with_memory_space_constraint(operand, pltpu.HBM) if spec is ANY else operand
                for operand, spec in zip(operands, in_specs)
            )
        )

    return pinned


def per_device(
    queries,
    new_kv,
    long_cache,
    short_cache,
    lengths,
    residual,
    out_weight,
    final_gain,
    head_weight,
    targets,
):
    row_count, heads = queries.shape[1], queries.shape[2]
    block_len, short_len = long_cache.shape[2], short_cache.shape[2]
    width, vocab = residual.shape[2], head_weight.shape[1]
    ctx_size, tp_size = lax.axis_size("ctx"), lax.axis_size("tp")
    chips = ctx_size // 2
    rows = 2 * row_count
    share = vocab // ctx_size
    padded = -(-(share + 1) // 128) * 128
    pairs = row_count * heads
    packed = HEAD_DIM // 2 + 8
    cores = [(i, i ^ 1) for i in range(ctx_size)]
    same_core = [list(range(which, ctx_size, 2)) for which in range(2)]

    flat_queries = queries.reshape(2, pairs, HEAD_DIM)
    long_rows = long_cache.reshape(2, row_count, block_len, HEAD_DIM)
    short_rows = short_cache.reshape(2, row_count, short_len, HEAD_DIM)
    fresh = new_kv.reshape(2, 2, row_count, HEAD_DIM)

    weight_rows = head_weight.T
    state = call(
        long_kernel,
        [((packed, 128), F32)],
        [ANY] * 3,
        "long_attention",
        [
            pltpu.SMEM((row_count,), jnp.int32),
            pltpu.VMEM((pairs, HEAD_DIM), BF16),
            pltpu.VMEM(long_rows.shape, BF16),
            pltpu.VMEM((pairs, HEAD_DIM), F32),
            pltpu.VMEM((pairs, HEAD_DIM), F32),
            pltpu.SemaphoreType.DMA((4,)),
        ],
        moved=2 * 1024 * 1024,
    )(lengths, flat_queries, long_rows)
    other = lax.ppermute(state, "ctx", cores)
    def ring(value, masks):
        return [
            lax.ppermute(value, "ctx", [(i, i ^ m) for i in range(ctx_size)]) for m in masks
        ]

    state = call(join_kernel, [((packed, 128), F32)], [VMEM] * 2, "merge_cores", flops=BESIDE)(
        state, other
    )
    near_y = ring(state, (2, 6, 4))
    state = call(join_kernel, [((packed, 128), F32)], [VMEM] * 4, "merge_y", flops=BESIDE)(
        state, *near_y
    )
    state, fresh = lax.optimization_barrier((state, fresh))
    near_x = ring(state, (8, 24, 16))
    aux, wanted, residual_near, gain_near = call(
        short_kernel,
        [
            ((3, pairs, HEAD_DIM), F32),
            ((rows, 128), jnp.int32),
            ((rows, width), BF16),
            ((1, width), F32),
        ],
        [VMEM] * 3 + [ANY] * 3,
        "short_attention",
        [pltpu.SMEM((row_count,), jnp.int32), pltpu.SemaphoreType.DMA((3,))],
        moved=1024 * 1024,
    )(
        flat_queries,
        short_rows,
        fresh,
        targets,
        residual.reshape(rows, width),
        final_gain.reshape(1, width),
    )
    spread = call(
        project_kernel, [((tp_size, rows, width), F32)], [VMEM] * 6, "project", flops=BESIDE
    )(state, *near_x, aux, out_weight)
    parts = lax.all_to_all(spread, "tp", 0, 0, tiled=True)

    theirs, scaled, squares = call(
        functools.partial(other_kernel, share),
        [((chips, rows, padded), F32), ((rows, width), BF16), ((rows, 128), F32)],
        [VMEM] * 4,
        "head_other",
        moved=4 * 1024 * 1024,
    )(parts, residual_near, gain_near, weight_rows)
    arrived = lax.ppermute(theirs, "ctx", cores)
    mine = call(
        functools.partial(same_kernel, share),
        [((chips, rows, padded), F32)],
        [VMEM] * 3,
        "head_same",
        moved=4 * 1024 * 1024,
    )(scaled, squares, weight_rows)
    blocks = call(add_kernel, [((chips, rows, padded), F32)], [VMEM] * 2, "add_cores")(
        mine, arrived
    )
    parts = lax.all_to_all(blocks, "ctx", 0, 0, tiled=True, axis_index_groups=same_core)

    devices = chips * tp_size
    logits, line = call(
        functools.partial(stats_kernel, share, vocab),
        [((rows, padded), F32), ((8, 128), F32)],
        [VMEM, VMEM],
        "vocab_stats",
    )(wanted, parts)
    arrived = lax.ppermute(line, "ctx", cores)
    spread = call(
        functools.partial(join_stats, rows), [((devices, 128), F32)], [VMEM] * 2, "join_stats"
    )(line, arrived)
    groups = [
        [c * tp_size + t for c in range(which, ctx_size, 2) for t in range(tp_size)]
        for which in range(2)
    ]
    everyone = lax.all_to_all(
        spread.reshape(devices, 1, 128), ("ctx", "tp"), 0, 0, tiled=True, axis_index_groups=groups
    ).reshape(devices, 128)
    scores, chosen = call(
        functools.partial(scores_kernel, share),
        [((row_count, share), F32), ((1, row_count), F32)],
        [VMEM, VMEM],
        "scores",
        near=jax.ShapeDtypeStruct,
    )(everyone, logits)
    return (scores, chosen.reshape(row_count))


def solution(mesh):
    placed = (
        P(None, None, "tp", None),
        P(None, None, None, "tp", None),
        P(None, None, "ctx", "tp", None),
        P(None, None, None, "tp", None),
        P(),
        P(None, None, "ctx"),
        P("tp", "ctx"),
        P("ctx"),
        P("ctx", "tp"),
        P(),
    )
    return jax.shard_map(
        per_device,
        mesh=mesh,
        in_specs=placed,
        out_specs=(P(None, ("tp", "ctx")), P()),
        check_vma=False,
    )
```
